256 devices in a mesh: dp: 32 (over x, z_hi, core), layer: 8 (over y, z_lo).
Axes of the slice: x: 4, y: 4, z: 8 (z_hi: 4, z_lo: 2; z = z_hi * 2 + z_lo), core: 2. Of those that a mesh axis runs over, the one named last changes fastest.
Arguments:
- grads: bfloat16 [8, 16384, 1024], P('layer', 'dp'), as said below
- damping_level: int32 [8], P('layer'), may hold values from 0 to 4, as said below
- pair_blocks: int32 [2048, 2], P('dp'), may hold values from -1 to 127, as said below
Outputs:
- tiles: float32 [2048, 128, 128], P(('dp', 'layer'))
The draws below stay inside these ranges and needn't reach their ends.
Inputs may be any that keep to these rules, and one draw needn't show every extreme that they name: `grads`: gradients of order one, finite. `damping_level`: consecutive layers have different levels. `pair_blocks`: row r is owned by shard r // 64, which holds blocks of that shard index times 4 onward; the first entry is one of the owner's blocks. The second is -1 for an empty slot, else a block of shard (owner + s) mod the number of dp shards with 1 <= s <= 4. The first slot of every owner is live with s = 4; the live slots of an owner come first, and some owner has no empty slot.
All inputs are finite; a program needn't handle non-finite values.
Results may differ from the reference program's by a relative error of at most 0.0042.
Values may be sent and summed in bfloat16 or wider, within the bound.
No kernel may reach another device: no remote copies, remote signals or barrier semaphores. Data moves between devices by JAX's collectives and lax.ppermute only.
A program may use at most 128 MiB of HBM per device.

```python
import math
import jax
import jax.numpy as jnp
from jax import lax

PROJ = 1024
BLOCK = 128
REACH = 4
BLK_DEV = 4
PAIR_DEV = 64
DOCS = 16384
BLOCKS = 128
LAYERS = 8
PAIRS = 2048


def draw_grads(key, part):
    key = jax.random.fold_in(key, 7)
    keys = jax.random.split(key, 2)
    col_scale = jnp.exp(jax.random.uniform(keys[1], (LAYERS, 1, PROJ), jnp.float32, -1.2, 1.2))
    row_scale = 0.6 + 1.2 * jnp.arange(DOCS, dtype=jnp.float32)[None, :, None] / DOCS
    noise = jnp.clip(jax.random.normal(keys[0], (LAYERS, DOCS, PROJ), jnp.float32), -6.0, 6.0)
    return (noise * col_scale * row_scale).astype(jnp.bfloat16)


def draw_damping_level(key, part):
    key = jax.random.fold_in(key, 13)
    keys = jax.random.split(key, 2)
    stride = jax.random.randint(keys[1], (), 1, 5, dtype=jnp.int32)
    position = jax.random.randint(keys[0], (), 0, LAYERS, dtype=jnp.int32)
    start = (4 - stride * position) % 5
    return ((start + stride * jnp.arange(LAYERS, dtype=jnp.int32)) % 5).astype(jnp.int32)


def draw_pair_blocks(key, part):
    key = jax.random.fold_in(key, 11)
    keys = jax.random.split(key, 5)
    shards = BLOCKS // BLK_DEV
    owner = jnp.arange(shards, dtype=jnp.int32)[:, None]
    within = jax.random.randint(keys[0], (shards, PAIR_DEV), 0, BLK_DEV, dtype=jnp.int32)
    distance = jax.random.randint(keys[1], (shards, PAIR_DEV), 1, REACH + 1, dtype=jnp.int32)
    distance = distance.at[:, 0].set(REACH)
    column = jax.random.randint(keys[2], (shards, PAIR_DEV), 0, BLK_DEV, dtype=jnp.int32)
    first_block = owner * BLK_DEV + within
    second_block = (owner + distance) % shards * BLK_DEV + column
    counts = jax.random.randint(keys[3], (shards,), PAIR_DEV // 4, PAIR_DEV + 1, dtype=jnp.int32)
    fullest = jax.random.randint(keys[4], (), 0, shards, dtype=jnp.int32)
    counts = jnp.where(jnp.arange(shards, dtype=jnp.int32) == fullest, PAIR_DEV, counts)
    live = jnp.arange(PAIR_DEV, dtype=jnp.int32)[None, :] < counts[:, None]
    second_block = jnp.where(live, second_block, -1)
    return jnp.stack([first_block, second_block], -1).reshape(PAIRS, 2).astype(jnp.int32)


def setup_inputs(seed: int = 0) -> dict:
    splits = jax.random.split(jax.random.key(seed), 4)
    grads = draw_grads(jax.random.fold_in(splits[3], 71), 0)
    damping_level = draw_damping_level(jax.random.fold_in(splits[3], 71), 0)
    pair_blocks = draw_pair_blocks(jax.random.fold_in(splits[3], 71), 0)
    return {"grads": grads, "damping_level": damping_level, "pair_blocks": pair_blocks}


def whiten_layer(layer_grads, level):
    damping = 0.05 * jnp.exp2(level.astype(jnp.float32))
    covariance = jnp.dot(layer_grads.T.astype(jnp.float32), layer_grads.astype(jnp.float32), preferred_element_type=jnp.float32) / DOCS
    covariance = covariance + damping * jnp.eye(PROJ, dtype=jnp.float32)
    factor = jnp.linalg.cholesky(covariance)
    solved = lax.linalg.triangular_solve(factor, layer_grads.astype(jnp.float32).T, left_side=True, lower=True)
    return solved.T.astype(jnp.bfloat16)

def reference(grads, damping_level, pair_blocks):
    whitened = lax.map(lambda item: whiten_layer(item[0], item[1]), (grads, damping_level))
    blocked = whitened.reshape(LAYERS, BLOCKS, BLOCK, PROJ)
    scale = 1.0 / math.sqrt(PROJ * LAYERS)

    def one_tile(pair):
        first_rows = blocked[:, pair[0]].astype(jnp.float32)
        second_rows = blocked[:, jnp.maximum(pair[1], 0)].astype(jnp.float32)
        product = jnp.einsum('lip,ljp->ij', first_rows, second_rows, precision=lax.Precision.HIGHEST)
        return jnp.where(pair[1] >= 0, product * scale, jnp.float32(0.0))
    return lax.map(one_tile, pair_blocks)
```

```python
import math

import jax
import jax.numpy as jnp
from jax import lax
from jax.experimental import pallas as pl
from jax.experimental.pallas import tpu as pltpu
from jax.sharding import PartitionSpec as P

BLOCK = 128
PIVOT = 256
PIVOTS = 4
WIDTH = PIVOT * PIVOTS
DOC_DEV = 512
DOCS = 16384
REACH = 4
HALF_ROWS = 18 * BLOCK
X_ROWS = HALF_ROWS // 4
Z_ROWS = X_ROWS // 4
SOURCES = 5
TOLERANCE = 3e-3
MAX_STEPS = 60
OFF_PLACE = {(1, 0): (0, 0), (2, 0): (0, 1), (3, 0): (0, 2), (2, 1): (1, 0), (3, 1): (1, 1), (3, 2): (1, 2)}

f32 = jnp.float32
bf16 = jnp.bfloat16


def dot(a, b, contract=((1,), (0,))):
    return lax.dot_general(
        a, b, (contract, ((), ())), precision=lax.Precision.HIGHEST, preferred_element_type=f32
    )


def dot16(a, b, contract=((1,), (0,))):
    return lax.dot_general(a, b, (contract, ((), ())), preferred_element_type=f32)


def move(value, dx=0, dz=0, dcore=0, chips=0):
    pairs = []
    for i in range(32):
        x, z, core = i // 8, (i // 2) % 4, i % 2
        chip = ((x + dx) % 4) * 4 + (z + dz) % 4
        pairs.append((i, ((chip + chips) % 16) * 2 + (core + dcore) % 2))
    return lax.ppermute(value, "dp", pairs)


def covariance_kernel(index_ref, g_ref, s_ref, out_ref):
    def product(place):
        i = pl.multiple_of(index_ref[2 * place] * PIVOT, PIVOT)
        j = pl.multiple_of(index_ref[2 * place + 1] * PIVOT, PIVOT)
        return dot16(g_ref[:, pl.ds(i, PIVOT)], g_ref[:, pl.ds(j, PIVOT)], ((0,), (0,))) + dot16(
            s_ref[:, pl.ds(i, PIVOT)], s_ref[:, pl.ds(j, PIVOT)], ((0,), (0,))
        )

    row = 0
    for place in range(5):
        block = product(place)
        for r, c in ((0, 0), (0, 1), (1, 0), (1, 1)):
            if place >= 3 and (r, c) == (0, 1):
                continue
            out_ref[row : row + BLOCK, :] = block[r * BLOCK : (r + 1) * BLOCK, c * BLOCK : (c + 1) * BLOCK]
            row += BLOCK


def covariance_half(g, sibling, core):
    first = jnp.array([1, 0, 2, 0, 3, 0, 0, 0, 1, 1], jnp.int32)
    second = jnp.array([2, 1, 3, 1, 3, 2, 2, 2, 3, 3], jnp.int32)
    index = jnp.where(core == 0, first, second)
    return pl.pallas_call(
        covariance_kernel,
        out_shape=jax.ShapeDtypeStruct((HALF_ROWS, BLOCK), f32),
        in_specs=[
            pl.BlockSpec(memory_space=pltpu.SMEM),
            pl.BlockSpec(memory_space=pltpu.VMEM),
            pl.BlockSpec(memory_space=pltpu.VMEM),
        ],
        out_specs=pl.BlockSpec(memory_space=pltpu.VMEM),
        compiler_params=pltpu.CompilerParams(vmem_limit_bytes=32 * 2**20),
        cost_estimate=pl.CostEstimate(flops=2 * 5 * PIVOT * PIVOT * 1024, bytes_accessed=4 * 2**20, transcendentals=0),
    )(index, g, sibling)


def norm(r):
    return jnp.max(jnp.sum(jnp.abs(r), axis=1, keepdims=True))


def invert(a, p_ref, m_ref, x_ref, r_ref):
    rows = lax.broadcasted_iota(jnp.int32, (PIVOT, PIVOT), 0)
    cols = lax.broadcasted_iota(jnp.int32, (PIVOT, PIVOT), 1)
    eye = jnp.where(rows == cols, 1.0, 0.0).astype(f32)
    diagonal = a * eye
    scale_row = lax.rsqrt(jnp.sum(diagonal, axis=0, keepdims=True))
    scale_col = lax.rsqrt(jnp.sum(diagonal, axis=1, keepdims=True))
    m = a * scale_row * scale_col
    m_ref[...] = m
    off = eye - m
    squared = dot(off, off)
    r_ref[...] = squared
    x_ref[...] = eye + off
    size = norm(squared)

    @pl.when(jnp.logical_not(size < 0.95))
    def _():
        step = 1.9 / norm(m)
        x = step * (2.0 * eye - step * m)
        x_ref[...] = x
        r_ref[...] = eye - dot(m, x)

    def unfinished(carry):
        size, count = carry
        return jnp.logical_and(size > TOLERANCE, count < MAX_STEPS)

    def improve(carry):
        _, count = carry
        x = x_ref[...] + dot(x_ref[...], r_ref[...])
        x_ref[...] = x
        r = eye - dot(m_ref[...], x)
        r_ref[...] = r
        return norm(r), count + 1

    lax.while_loop(unfinished, improve, (norm(r_ref[...]), jnp.int32(0)))
    x = x_ref[...] + dot(x_ref[...], r_ref[...])
    p_ref[...] = x * scale_row * scale_col


def solve_kernel(place_ref, level_ref, w_ref, s_ref, g_ref, out_ref, packed, c, low, p, y, m, x, r):
    mine_x, mine_z, core = place_ref[0], place_ref[1], place_ref[2]
    for half, ref in ((core, w_ref), (1 - core, s_ref)):
        for i in range(4):
            for j in range(4):
                row = half * HALF_ROWS + ((mine_x + i) % 4) * X_ROWS + ((mine_z + j) % 4) * Z_ROWS
                row = pl.multiple_of(row, 16)
                start = i * X_ROWS + j * Z_ROWS
                packed[pl.ds(row, Z_ROWS), :] = ref[start : start + Z_ROWS, :]

    rows = lax.broadcasted_iota(jnp.int32, (PIVOT, PIVOT), 0)
    cols = lax.broadcasted_iota(jnp.int32, (PIVOT, PIVOT), 1)
    level = jnp.full((PIVOT, PIVOT), level_ref[0], jnp.int32).astype(f32)
    damped = jnp.where(rows == cols, 0.05 * jnp.exp2(level), 0.0)

    def piece(half, place):
        start = half * HALF_ROWS + place * BLOCK
        return packed[start : start + BLOCK, :] * (1.0 / DOCS)

    for (i, j), (half, place) in OFF_PLACE.items():
        for t in range(4):
            c[i, j, (t // 2) * BLOCK : (t // 2 + 1) * BLOCK, (t % 2) * BLOCK : (t % 2 + 1) * BLOCK] = piece(
                half, 4 * place + t
            )
    for i in range(PIVOTS):
        half, place = i // 2, 12 + 3 * (i % 2)
        a, b, d = piece(half, place), piece(half, place + 1), piece(half, place + 2)
        top = jnp.concatenate([a, b.T], axis=1)
        bottom = jnp.concatenate([b, d], axis=1)
        c[i, i] = jnp.concatenate([top, bottom], axis=0) + damped
    for i in range(PIVOTS):
        y[i] = g_ref[:, i * PIVOT : (i + 1) * PIVOT].astype(f32)

    for k in range(PIVOTS):
        invert(c[k, k], p.at[k], m, x, r)
        for i in range(k + 1, PIVOTS):
            low[i, k] = dot(c[i, k], p[k])
        for i in range(k + 1, PIVOTS):
            for j in range(k + 1, i + 1):
                c[i, j] = c[i, j] - dot(low[i, k], c[j, k], ((1,), (1,)))
        for i in range(k + 1, PIVOTS):
            y[i] = y[i] - dot(y[k], low[i, k], ((1,), (1,)))
    scale = 1.0 / math.sqrt(WIDTH * 8)
    for k in range(PIVOTS - 1, -1, -1):
        h = dot(y[k], p[k])
        for i in range(k + 1, PIVOTS):
            h = h - dot(y[i], low[i, k])
        y[k] = h
        h = h * scale
        high = h.astype(bf16)
        rest = (h - high.astype(f32)).astype(bf16)
        for block in range(DOC_DEV // BLOCK):
            out_ref[block, :BLOCK, k * PIVOT : (k + 1) * PIVOT] = high[block * BLOCK : (block + 1) * BLOCK]
            out_ref[block, BLOCK:, k * PIVOT : (k + 1) * PIVOT] = rest[block * BLOCK : (block + 1) * BLOCK]


def solve(place, level, mine, other, g):
    smem, vmem = pl.BlockSpec(memory_space=pltpu.SMEM), pl.BlockSpec(memory_space=pltpu.VMEM)
    return pl.pallas_call(
        solve_kernel,
        out_shape=jax.ShapeDtypeStruct((DOC_DEV // BLOCK, 2 * BLOCK, WIDTH), bf16),
        in_specs=[smem, smem, vmem, vmem, vmem],
        out_specs=vmem,
        scratch_shapes=[
            pltpu.VMEM((2 * HALF_ROWS, BLOCK), f32),
            pltpu.VMEM((PIVOTS, PIVOTS, PIVOT, PIVOT), f32),
            pltpu.VMEM((PIVOTS, PIVOTS, PIVOT, PIVOT), f32),
            pltpu.VMEM((PIVOTS, PIVOT, PIVOT), f32),
            pltpu.VMEM((PIVOTS, DOC_DEV, PIVOT), f32),
            pltpu.VMEM((PIVOT, PIVOT), f32),
            pltpu.VMEM((PIVOT, PIVOT), f32),
            pltpu.VMEM((PIVOT, PIVOT), f32),
        ],
        compiler_params=pltpu.CompilerParams(vmem_limit_bytes=48 * 2**20),
        cost_estimate=pl.CostEstimate(flops=40 * 10**9, bytes_accessed=8 * 2**20, transcendentals=0),
    )(place, level, mine, other, g)


def tiles_kernel(pairs_ref, h_ref, *refs):
    sources, (out_ref, held, sems) = refs[:SOURCES], refs[SOURCES:]
    copies = [
        pltpu.make_async_copy(source, held.at[pl.ds(n * DOC_DEV, DOC_DEV)], sems.at[n])
        for n, source in enumerate(sources)
    ]
    for copy in copies:
        copy.start()
    for copy in copies:
        copy.wait()

    def one(n, carry):
        first, second, live = pairs_ref[0, n], pairs_ref[1, n], pairs_ref[2, n]
        partner = held[pl.ds(pl.multiple_of(second * BLOCK, BLOCK), BLOCK), :]
        both = dot16(h_ref[first], partner, ((1,), (1,)))
        tile = both[:BLOCK] + both[BLOCK:]
        out_ref[n] = jnp.where(live > 0, tile, 0.0).astype(bf16)
        return carry

    lax.fori_loop(0, out_ref.shape[0], one, 0, unroll=4)


def layer_tiles(pairs, h, sources):
    count = pairs.shape[1]
    return pl.pallas_call(
        tiles_kernel,
        out_shape=jax.ShapeDtypeStruct((count, BLOCK, BLOCK), bf16),
        in_specs=[pl.BlockSpec(memory_space=pltpu.SMEM), pl.BlockSpec(memory_space=pltpu.VMEM)]
        + [pl.BlockSpec(memory_space=pl.ANY)] * SOURCES,
        out_specs=pl.BlockSpec(memory_space=pltpu.VMEM),
        scratch_shapes=[pltpu.VMEM((SOURCES * DOC_DEV, WIDTH), bf16), pltpu.SemaphoreType.DMA((SOURCES,))],
        compiler_params=pltpu.CompilerParams(vmem_limit_bytes=32 * 2**20),
        cost_estimate=pl.CostEstimate(
            flops=4 * count * BLOCK * BLOCK * WIDTH, bytes_accessed=9 * 2**20, transcendentals=0
        ),
    )(pairs, h, *sources)


def shards(grads, damping_level, pair_blocks):
    g = grads[0]
    me = lax.axis_index("dp")
    mine_x, mine_z, core = me // 8, (me // 2) % 4, me % 2
    sibling = move(g, dcore=1)
    near = move(g, chips=-1)
    far = move(near, chips=-1)
    near_other = move(near, dcore=1)
    far_other = move(far, dcore=1)

    part = covariance_half(g, sibling, core)
    for position, rows, axis in ((mine_x, X_ROWS, "dx"), (mine_z, Z_ROWS, "dz")):
        cut = [lax.dynamic_slice_in_dim(part, ((position + s) % 4) * rows, rows) for s in range(4)]
        part = cut[0] + move(cut[1], **{axis: 1}) + move(cut[2], **{axis: 2}) + move(cut[3], **{axis: 3})
    for axis in ("dz", "dx"):
        part = jnp.concatenate([part] + [move(part, **{axis: -s}) for s in (1, 2, 3)])
    other = move(part, dcore=1)
    place = jnp.stack([mine_x, mine_z, core]).astype(jnp.int32)
    h = solve(place, damping_level, part, other, g)

    blocks_dev = DOC_DEV // BLOCK
    first, second = pair_blocks[:, 0], pair_blocks[:, 1]
    live = second >= 0
    second = jnp.maximum(second, 0)
    distance = jnp.clip((second // blocks_dev - me) % 32, 1, REACH) - 1
    source = jnp.where(core == 0, jnp.array([0, 1, 2, 3]), jnp.array([2, 1, 4, 3]))
    held_block = source[distance] * blocks_dev + second % blocks_dev
    pairs = jnp.stack([first - me * blocks_dev, held_block, live.astype(jnp.int32)]).astype(jnp.int32)
    terms = layer_tiles(pairs, h, (sibling, near, near_other, far, far_other))
    terms = lax.all_to_all(terms.reshape(8, -1, BLOCK, BLOCK), "layer", 0, 0)
    return jnp.sum(terms.astype(f32), axis=0)


def solution(mesh):
    return jax.shard_map(
        shards,
        mesh=mesh,
        in_specs=(P("layer", "dp", None), P("layer"), P("dp", None)),
        out_specs=P(("dp", "layer"), None, None),
        check_vma=False,
    )
```

```python
import math

import jax
import jax.numpy as jnp
from jax import lax
from jax.experimental import pallas as pl
from jax.experimental.pallas import tpu as pltpu
from jax.sharding import PartitionSpec as P

BLOCK = 128
PIVOT = 256
PIVOTS = 4
WIDTH = PIVOT * PIVOTS
DOC_DEV = 512
DOCS = 16384
REACH = 4
HALF_ROWS = 18 * BLOCK
X_ROWS = HALF_ROWS // 4
Z_ROWS = X_ROWS // 4
SOURCES = 5
TOLERANCE = 0.03
MAX_STEPS = 60
OFF_PLACE = {(1, 0): (0, 0), (2, 0): (0, 1), (3, 0): (0, 2), (2, 1): (1, 0), (3, 1): (1, 1), (3, 2): (1, 2)}

f32 = jnp.float32
bf16 = jnp.bfloat16


def dot(a, b, contract=((1,), (0,))):
    return lax.dot_general(
        a, b, (contract, ((), ())), precision=lax.Precision.HIGHEST, preferred_element_type=f32
    )


def dot16(a, b, contract=((1,), (0,))):
    return lax.dot_general(a, b, (contract, ((), ())), preferred_element_type=f32)


def split(value):
    high = value.astype(bf16)
    return high, (value - high.astype(f32)).astype(bf16)


def dot3(a, b, contract=((1,), (0,))):
    (a_high, a_low), (b_high, b_low) = a, b
    return dot16(a_high, b_high, contract) + (dot16(a_high, b_low, contract) + dot16(a_low, b_high, contract))


def split(value):
    high = value.astype(bf16)
    return high, (value - high.astype(f32)).astype(bf16)


def dot3(a, b, contract=((1,), (0,))):
    (a_high, a_low), (b_high, b_low) = a, b
    return dot16(a_high, b_high, contract) + (dot16(a_high, b_low, contract) + dot16(a_low, b_high, contract))


def move(value, dx=0, dz=0, dcore=0, chips=0):
    pairs = []
    for i in range(32):
        x, z, core = i // 8, (i // 2) % 4, i % 2
        chip = ((x + dx) % 4) * 4 + (z + dz) % 4
        pairs.append((i, ((chip + chips) % 16) * 2 + (core + dcore) % 2))
    return lax.ppermute(value, "dp", pairs)


def move_up(value):
    pairs = []
    for i in range(32):
        x, z, core = i // 8, (i // 2) % 4, i % 2
        pairs.append((i, ((x - (z < 2)) % 4) * 8 + (z + 1) % 4 * 2 + core))
    return lax.ppermute(value, "dp", pairs)


def carry(value):
    pairs = []
    for i in range(32):
        x, z, core = i // 8, (i // 2) % 4, i % 2
        pairs.append((i, ((x - (z == 0)) % 4) * 8 + z * 2 + core))
    return lax.ppermute(value, "dp", pairs)


def covariance_kernel(index_ref, g_ref, s_ref, out_ref):
    def product(place):
        i = pl.multiple_of(index_ref[2 * place] * PIVOT, PIVOT)
        j = pl.multiple_of(index_ref[2 * place + 1] * PIVOT, PIVOT)
        return dot16(g_ref[:, pl.ds(i, PIVOT)], g_ref[:, pl.ds(j, PIVOT)], ((0,), (0,))) + dot16(
            s_ref[:, pl.ds(i, PIVOT)], s_ref[:, pl.ds(j, PIVOT)], ((0,), (0,))
        )

    row = 0
    for place in range(5):
        block = product(place)
        for r, c in ((0, 0), (0, 1), (1, 0), (1, 1)):
            if place >= 3 and (r, c) == (0, 1):
                continue
            out_ref[row : row + BLOCK, :] = block[r * BLOCK : (r + 1) * BLOCK, c * BLOCK : (c + 1) * BLOCK]
            row += BLOCK


def covariance_half(g, sibling, core):
    first = jnp.array([1, 0, 2, 0, 3, 0, 0, 0, 1, 1], jnp.int32)
    second = jnp.array([2, 1, 3, 1, 3, 2, 2, 2, 3, 3], jnp.int32)
    index = jnp.where(core == 0, first, second)
    return pl.pallas_call(
        covariance_kernel,
        out_shape=jax.ShapeDtypeStruct((HALF_ROWS, BLOCK), f32),
        in_specs=[
            pl.BlockSpec(memory_space=pltpu.SMEM),
            pl.BlockSpec(memory_space=pltpu.VMEM),
            pl.BlockSpec(memory_space=pltpu.VMEM),
        ],
        out_specs=pl.BlockSpec(memory_space=pltpu.VMEM),
        compiler_params=pltpu.CompilerParams(vmem_limit_bytes=32 * 2**20),
        cost_estimate=pl.CostEstimate(flops=10**6, bytes_accessed=2**10, transcendentals=0),
    )(index, g, sibling)


def norm(r):
    return jnp.max(jnp.sum(jnp.abs(r), axis=1, keepdims=True))


def invert(a, p_ref, m_ref, x_ref, r_ref):
    rows = lax.broadcasted_iota(jnp.int32, (PIVOT, PIVOT), 0)
    cols = lax.broadcasted_iota(jnp.int32, (PIVOT, PIVOT), 1)
    eye = jnp.where(rows == cols, 1.0, 0.0).astype(f32)
    diagonal = a * eye
    scale_row = lax.rsqrt(jnp.sum(diagonal, axis=0, keepdims=True))
    scale_col = lax.rsqrt(jnp.sum(diagonal, axis=1, keepdims=True))
    m = a * scale_row * scale_col
    m_ref[...] = m
    off = eye - m
    halves = split(off)
    squared = dot3(halves, halves)
    x_ref[...] = eye + off + (squared + dot3(halves, split(squared)))

    @pl.when(jnp.logical_not(norm(squared) < 0.95))
    def _():
        step = 1.9 / norm(m_ref[...])
        x_ref[...] = step * (2.0 * eye - step * m_ref[...])

    def residual():
        r = eye - dot(m_ref[...], x_ref[...])
        r_ref[...] = r
        return norm(r)

    def unfinished(carry):
        size, count = carry
        return jnp.logical_and(size > TOLERANCE, count < MAX_STEPS)

    def improve(carry):
        x_ref[...] = x_ref[...] + dot(x_ref[...], r_ref[...])
        return residual(), carry[1] + 1

    lax.while_loop(unfinished, improve, (residual(), jnp.int32(0)))
    r = split(r_ref[...])
    first = dot3(split(x_ref[...]), r)
    x = x_ref[...] + (first + dot3(split(first), r))
    p_ref[...] = x * scale_row * scale_col


def solve_kernel(place_ref, level_ref, *refs):
    parts, others, g_ref, out_ref = refs[:4], refs[4:8], refs[8], refs[9]
    packed, c, low, low_high, low_low, p, y, m, x, r = refs[10:]
    mine_x, mine_z, core = place_ref[0], place_ref[1], place_ref[2]
    for half, group in ((core, parts), (1 - core, others)):
        for i in range(4):
            for j in range(4):
                row = half * HALF_ROWS + ((mine_x + i) % 4) * X_ROWS + ((mine_z + j) % 4) * Z_ROWS
                row = pl.multiple_of(row, 16)
                packed[pl.ds(row, Z_ROWS), :] = group[i][j * Z_ROWS : (j + 1) * Z_ROWS, :]

    rows = lax.broadcasted_iota(jnp.int32, (PIVOT, PIVOT), 0)
    cols = lax.broadcasted_iota(jnp.int32, (PIVOT, PIVOT), 1)
    level = jnp.full((PIVOT, PIVOT), level_ref[0], jnp.int32).astype(f32)
    damped = jnp.where(rows == cols, 0.05 * jnp.exp2(level), 0.0)

    def piece(half, place):
        start = half * HALF_ROWS + place * BLOCK
        return packed[start : start + BLOCK, :] * (1.0 / DOCS)

    for (i, j), (half, place) in OFF_PLACE.items():
        for t in range(4):
            c[i, j, (t // 2) * BLOCK : (t // 2 + 1) * BLOCK, (t % 2) * BLOCK : (t % 2 + 1) * BLOCK] = piece(
                half, 4 * place + t
            )
    for i in range(PIVOTS):
        half, place = i // 2, 12 + 3 * (i % 2)
        a, b, d = piece(half, place), piece(half, place + 1), piece(half, place + 2)
        top = jnp.concatenate([a, b.T], axis=1)
        bottom = jnp.concatenate([b, d], axis=1)
        c[i, i] = jnp.concatenate([top, bottom], axis=0) + damped
    for i in range(PIVOTS):
        y[i] = g_ref[:, i * PIVOT : (i + 1) * PIVOT].astype(f32)

    for k in range(PIVOTS):
        invert(c[k, k], p.at[k], m, x, r)
        for i in range(k + 1, PIVOTS):
            value = dot(c[i, k], p[k])
            low[i, k] = value
            low_high[i, k], low_low[i, k] = split(value)
        for i in range(k + 1, PIVOTS):
            for j in range(k + 1, i + 1):
                c[i, j] = c[i, j] - dot(low[i, k], c[j, k], ((1,), (1,)))
        halves = split(y[k])
        for i in range(k + 1, PIVOTS):
            y[i] = y[i] - dot3(halves, (low_high[i, k], low_low[i, k]), ((1,), (1,)))
    scale = 1.0 / math.sqrt(WIDTH * 8)
    solved = {}
    for k in range(PIVOTS - 1, -1, -1):
        h = dot3(split(y[k]), split(p[k]))
        for i in range(k + 1, PIVOTS):
            h = h - dot3(solved[i], (low_high[i, k], low_low[i, k]))
        solved[k] = split(h)
        h = h * scale
        high = h.astype(bf16)
        rest = (h - high.astype(f32)).astype(bf16)
        for block in range(DOC_DEV // BLOCK):
            out_ref[2 * block * BLOCK : (2 * block + 1) * BLOCK, k * PIVOT : (k + 1) * PIVOT] = high[block * BLOCK : (block + 1) * BLOCK]
            out_ref[(2 * block + 1) * BLOCK : (2 * block + 2) * BLOCK, k * PIVOT : (k + 1) * PIVOT] = rest[block * BLOCK : (block + 1) * BLOCK]


def solve(place, level, mine, other, g):
    smem, vmem = pl.BlockSpec(memory_space=pltpu.SMEM), pl.BlockSpec(memory_space=pltpu.VMEM)
    return pl.pallas_call(
        solve_kernel,
        out_shape=jax.ShapeDtypeStruct((2 * DOC_DEV, WIDTH), bf16),
        in_specs=[smem, smem] + [vmem] * 9,
        out_specs=vmem,
        scratch_shapes=[
            pltpu.VMEM((2 * HALF_ROWS, BLOCK), f32),
            pltpu.VMEM((PIVOTS, PIVOTS, PIVOT, PIVOT), f32),
            pltpu.VMEM((PIVOTS, PIVOTS, PIVOT, PIVOT), f32),
            pltpu.VMEM((PIVOTS, PIVOTS, PIVOT, PIVOT), bf16),
            pltpu.VMEM((PIVOTS, PIVOTS, PIVOT, PIVOT), bf16),
            pltpu.VMEM((PIVOTS, PIVOT, PIVOT), f32),
            pltpu.VMEM((PIVOTS, DOC_DEV, PIVOT), f32),
            pltpu.VMEM((PIVOT, PIVOT), f32),
            pltpu.VMEM((PIVOT, PIVOT), f32),
            pltpu.VMEM((PIVOT, PIVOT), f32),
        ],
        compiler_params=pltpu.CompilerParams(vmem_limit_bytes=48 * 2**20),
        cost_estimate=pl.CostEstimate(flops=10**6, bytes_accessed=2**10, transcendentals=0),
    )(place, level, *mine, *other, g)


def tiles_kernel(pairs_ref, place_ref, h_ref, *refs):
    core = place_ref[2]
    me = place_ref[0] * 8 + place_ref[1] * 2 + core
    pieces, (out_ref, held, joined) = refs[:7], refs[7:]
    for n in range(2):
        near, last, far = pieces[3 * n + 1 : 3 * n + 4]
        joined[2 * n, :320, :] = near[...]
        joined[2 * n, 320:, :] = last[:192, :]
        joined[2 * n + 1, :192, :] = last[192:, :]
        joined[2 * n + 1, 192:, :] = far[...]

    def fill(n):
        for start in range(0, DOC_DEV, 2 * BLOCK):
            rows = pieces[0][start : start + 2 * BLOCK, :] if n == 0 else joined[n - 1, start : start + 2 * BLOCK, :]
            both = dot16(h_ref[...], rows, ((1,), (1,)))
            for a in range(DOC_DEV // BLOCK):
                tile = both[2 * a * BLOCK : (2 * a + 1) * BLOCK] + both[(2 * a + 1) * BLOCK : (2 * a + 2) * BLOCK]
                tile = tile.astype(bf16)
                place = (n * DOC_DEV + start) // BLOCK
                held[a, place] = tile[:, :BLOCK]
                held[a, place + 1] = tile[:, BLOCK:]

    pl.when(core == 0)(lambda: fill(0))
    pl.when(core == 1)(lambda: fill(SOURCES - 1))
    for n in range(1, SOURCES - 1):
        fill(n)

    blocks = DOC_DEV // BLOCK

    def one(n, carry):
        first, second = pairs_ref[2 * n] - me * blocks, pairs_ref[2 * n + 1]
        ahead = jnp.maximum(second, 0) - me * blocks
        ahead = jnp.where(ahead < 0, ahead + 32 * blocks, ahead)
        distance = jnp.clip(lax.shift_right_logical(ahead, 2), 1, REACH)
        even = jnp.where(distance == 1, 0, jnp.where(distance == 2, 1, jnp.where(distance == 3, 3, 2)))
        odd = jnp.where(distance == 1, 3, jnp.where(distance == 2, 1, jnp.where(distance == 3, 4, 2)))
        source = jnp.where(core == 0, even, odd)
        tile = held[first, source * blocks + jnp.bitwise_and(ahead, 3)]
        out_ref[n] = jnp.where(second >= 0, tile, jnp.zeros_like(tile))
        return carry

    lax.fori_loop(0, out_ref.shape[0], one, 0, unroll=4)


def layer_tiles(pairs, place, h, pieces):
    count = pairs.shape[0] // 2
    vmem, smem = pl.BlockSpec(memory_space=pltpu.VMEM), pl.BlockSpec(memory_space=pltpu.SMEM)
    return pl.pallas_call(
        tiles_kernel,
        out_shape=jax.ShapeDtypeStruct((count, BLOCK, BLOCK), bf16),
        in_specs=[smem, smem] + [vmem] * (1 + len(pieces)),
        out_specs=vmem,
        scratch_shapes=[
            pltpu.VMEM((DOC_DEV // BLOCK, SOURCES * DOC_DEV // BLOCK, BLOCK, BLOCK), bf16),
            pltpu.VMEM((SOURCES - 1, DOC_DEV, WIDTH), bf16),
        ],
        compiler_params=pltpu.CompilerParams(vmem_limit_bytes=32 * 2**20),
        cost_estimate=pl.CostEstimate(
            flops=4 * count * BLOCK * BLOCK * WIDTH, bytes_accessed=9 * 2**20, transcendentals=0
        ),
    )(pairs, place, h, *pieces)


def scatter(part, position, rows, axis):
    cut = [lax.dynamic_slice_in_dim(part, ((position + s) % 4) * rows, rows) for s in range(4)]
    return [cut[0]] + [move(cut[s], **{axis: s}) for s in (1, 2, 3)]


def gather(part, axis):
    return [part] + [move(part, **{axis: -s}) for s in (1, 2, 3)]


def shards(grads, damping_level, pair_blocks):
    g = grads[0]
    me = lax.axis_index("dp")
    mine_x, mine_z, core = me // 8, (me // 2) % 4, me % 2
    near_0 = move(g[:320], chips=-1)
    turned = move_up(g[192:])
    sibling = move(g, dcore=1)

    part = covariance_half(g, sibling, core)
    cut = scatter(part, mine_x, X_ROWS, "dx")
    *cut, near_0, turned, rest = lax.optimization_barrier((*cut, near_0, turned, g))
    last = carry(jnp.concatenate([rest[320:], near_0[:192]]))
    cut = scatter(cut[0] + cut[1] + cut[2] + cut[3], mine_z, Z_ROWS, "dz")
    part = jnp.concatenate(gather(cut[0] + cut[1] + cut[2] + cut[3], "dz"))
    part, near_0, turned, last = lax.optimization_barrier((part, near_0, turned, last))
    last = move(last, dz=-1)
    far_up = move(turned, dz=1)
    near_0_other = move(near_0, dcore=1)
    parts = gather(part, "dx")
    others = [move(part, dcore=1) for part in parts]
    place = jnp.stack([mine_x, mine_z, core]).astype(jnp.int32)
    h = solve(place, damping_level, parts, others, g)
    h, last, far_up = lax.optimization_barrier((h, last, far_up))
    last_other, far_up_other = move(last, dcore=1), move(far_up, dcore=1)

    pieces = (sibling, near_0, last, far_up, near_0_other, last_other, far_up_other)
    terms = layer_tiles(pair_blocks.reshape(-1), place, h, pieces)
    terms = lax.all_to_all(terms.reshape(8, -1, BLOCK, BLOCK), "layer", 0, 0)
    return jnp.sum(terms.astype(f32), axis=0)


def solution(mesh):
    return jax.shard_map(
        shards,
        mesh=mesh,
        in_specs=(P("layer", "dp", None), P("layer"), P("dp", None)),
        out_specs=P(("dp", "layer"), None, None),
        check_vma=False,
    )
```

```python
import math

import jax
import jax.numpy as jnp
from jax import lax
from jax.experimental import pallas as pl
from jax.experimental.pallas import tpu as pltpu
from jax.sharding import PartitionSpec as P

BLOCK = 128
PIVOT = 256
PIVOTS = 4
WIDTH = PIVOT * PIVOTS
DOC_DEV = 512
DOCS = 16384
REACH = 4
HALF_ROWS = 18 * BLOCK
X_ROWS = HALF_ROWS // 4
Z_ROWS = X_ROWS // 4
BLOCKS_DEV = 4
NEAR = 320
EARLY = 192
UP = 192
TOLERANCE = 0.03
MAX_STEPS = 60
OFF_PLACE = {(1, 0): (0, 0), (2, 0): (0, 1), (3, 0): (0, 2), (2, 1): (1, 0), (3, 1): (1, 1), (3, 2): (1, 2)}

f32 = jnp.float32
bf16 = jnp.bfloat16


def dot(a, b, contract=((1,), (0,))):
    return lax.dot_general(
        a, b, (contract, ((), ())), precision=lax.Precision.HIGHEST, preferred_element_type=f32
    )


def dot16(a, b, contract=((1,), (0,))):
    return lax.dot_general(a, b, (contract, ((), ())), preferred_element_type=f32)


def split(value):
    high = value.astype(bf16)
    return high, (value - high.astype(f32)).astype(bf16)


def dot3(a, b, contract=((1,), (0,))):
    (a_high, a_low), (b_high, b_low) = a, b
    return dot16(a_high, b_high, contract) + (dot16(a_high, b_low, contract) + dot16(a_low, b_high, contract))


def split(value):
    high = value.astype(bf16)
    return high, (value - high.astype(f32)).astype(bf16)


def dot3(a, b, contract=((1,), (0,))):
    (a_high, a_low), (b_high, b_low) = a, b
    return dot16(a_high, b_high, contract) + (dot16(a_high, b_low, contract) + dot16(a_low, b_high, contract))


def move(value, dx=0, dz=0, dcore=0, chips=0):
    pairs = []
    for i in range(32):
        x, z, core = i // 8, (i // 2) % 4, i % 2
        chip = ((x + dx) % 4) * 4 + (z + dz) % 4
        pairs.append((i, ((chip + chips) % 16) * 2 + (core + dcore) % 2))
    return lax.ppermute(value, "dp", pairs)


def move_up(value):
    pairs = []
    for i in range(32):
        x, z, core = i // 8, (i // 2) % 4, i % 2
        pairs.append((i, ((x - (z < 2)) % 4) * 8 + (z + 1) % 4 * 2 + core))
    return lax.ppermute(value, "dp", pairs)


def carry(value):
    pairs = []
    for i in range(32):
        x, z, core = i // 8, (i // 2) % 4, i % 2
        pairs.append((i, ((x - (z == 0)) % 4) * 8 + z * 2 + core))
    return lax.ppermute(value, "dp", pairs)


def move_layer(value, dy=0, dz=0):
    pairs = [(i, ((i // 2 + dy) % 4) * 2 + (i + dz) % 2) for i in range(8)]
    return lax.ppermute(value, "layer", pairs)


def covariance_kernel(index_ref, g_ref, s_ref, out_ref):
    def product(place):
        i = pl.multiple_of(index_ref[2 * place] * PIVOT, PIVOT)
        j = pl.multiple_of(index_ref[2 * place + 1] * PIVOT, PIVOT)
        return dot16(g_ref[:, pl.ds(i, PIVOT)], g_ref[:, pl.ds(j, PIVOT)], ((0,), (0,))) + dot16(
            s_ref[:, pl.ds(i, PIVOT)], s_ref[:, pl.ds(j, PIVOT)], ((0,), (0,))
        )

    row = 0
    for place in range(5):
        block = product(place)
        for r, c in ((0, 0), (0, 1), (1, 0), (1, 1)):
            if place >= 3 and (r, c) == (0, 1):
                continue
            out_ref[row : row + BLOCK, :] = block[r * BLOCK : (r + 1) * BLOCK, c * BLOCK : (c + 1) * BLOCK]
            row += BLOCK


def covariance_half(g, sibling, core):
    first = jnp.array([1, 0, 2, 0, 3, 0, 0, 0, 1, 1], jnp.int32)
    second = jnp.array([2, 1, 3, 1, 3, 2, 2, 2, 3, 3], jnp.int32)
    index = jnp.where(core == 0, first, second)
    return pl.pallas_call(
        covariance_kernel,
        out_shape=jax.ShapeDtypeStruct((HALF_ROWS, BLOCK), f32),
        in_specs=[
            pl.BlockSpec(memory_space=pltpu.SMEM),
            pl.BlockSpec(memory_space=pltpu.VMEM),
            pl.BlockSpec(memory_space=pltpu.VMEM),
        ],
        out_specs=pl.BlockSpec(memory_space=pltpu.VMEM),
        compiler_params=pltpu.CompilerParams(vmem_limit_bytes=12 * 2**20),
        cost_estimate=pl.CostEstimate(flops=10**6, bytes_accessed=2**10, transcendentals=0),
    )(index, g, sibling)


def norm(r):
    return jnp.max(jnp.sum(jnp.abs(r), axis=1, keepdims=True))


def invert(a, p_ref, m_ref, x_ref, r_ref):
    rows = lax.broadcasted_iota(jnp.int32, (PIVOT, PIVOT), 0)
    cols = lax.broadcasted_iota(jnp.int32, (PIVOT, PIVOT), 1)
    eye = jnp.where(rows == cols, 1.0, 0.0).astype(f32)
    diagonal = a * eye
    scale_row = lax.rsqrt(jnp.sum(diagonal, axis=0, keepdims=True))
    scale_col = lax.rsqrt(jnp.sum(diagonal, axis=1, keepdims=True))
    m = a * scale_row * scale_col
    m_ref[...] = m
    off = eye - m
    halves = split(off)
    squared = dot3(halves, halves)
    x_ref[...] = eye + off + (squared + dot3(halves, split(squared)))

    def residual():
        r = eye - dot(m_ref[...], x_ref[...])
        r_ref[...] = r
        return norm(r)

    size = residual()

    @pl.when(jnp.logical_not(size <= TOLERANCE))
    def _():
        @pl.when(jnp.logical_not(size < 0.9))
        def _():
            step = 1.9 / norm(m_ref[...])
            x_ref[...] = step * (2.0 * eye - step * m_ref[...])

        def unfinished(carry):
            size, count = carry
            return jnp.logical_and(size > TOLERANCE, count < MAX_STEPS)

        def improve(carry):
            x_ref[...] = x_ref[...] + dot(x_ref[...], r_ref[...])
            return residual(), carry[1] + 1

        lax.while_loop(unfinished, improve, (residual(), jnp.int32(0)))

    r = split(r_ref[...])
    first = dot3(split(x_ref[...]), r)
    x = x_ref[...] + (first + dot3(split(first), r))
    p_ref[...] = x * scale_row * scale_col


def spot(i, j):
    return i * (i + 1) // 2 + j


def solve_kernel(place_ref, level_ref, *refs):
    parts, others, g_ref, out_ref = refs[:4], refs[4:8], refs[8], refs[9]
    packed, c, low_high, low_low, p, y, m, x, r = refs[10:]
    low = {}
    mine_x, mine_z, core = place_ref[0], place_ref[1], place_ref[2]
    for half, group in ((core, parts), (1 - core, others)):
        for i in range(4):
            for j in range(4):
                row = half * HALF_ROWS + ((mine_x + i) % 4) * X_ROWS + ((mine_z + j) % 4) * Z_ROWS
                row = pl.multiple_of(row, 16)
                packed[pl.ds(row, Z_ROWS), :] = group[i][j * Z_ROWS : (j + 1) * Z_ROWS, :]

    rows = lax.broadcasted_iota(jnp.int32, (PIVOT, PIVOT), 0)
    cols = lax.broadcasted_iota(jnp.int32, (PIVOT, PIVOT), 1)
    level = jnp.full((PIVOT, PIVOT), level_ref[0], jnp.int32).astype(f32)
    damped = jnp.where(rows == cols, 0.05 * jnp.exp2(level), 0.0)

    def piece(half, place):
        start = half * HALF_ROWS + place * BLOCK
        return packed[start : start + BLOCK, :] * (1.0 / DOCS)

    for (i, j), (half, place) in OFF_PLACE.items():
        for t in range(4):
            c[spot(i, j), (t // 2) * BLOCK : (t // 2 + 1) * BLOCK, (t % 2) * BLOCK : (t % 2 + 1) * BLOCK] = piece(
                half, 4 * place + t
            )
    for i in range(PIVOTS):
        half, place = i // 2, 12 + 3 * (i % 2)
        a, b, d = piece(half, place), piece(half, place + 1), piece(half, place + 2)
        top = jnp.concatenate([a, b.T], axis=1)
        bottom = jnp.concatenate([b, d], axis=1)
        c[spot(i, i)] = jnp.concatenate([top, bottom], axis=0) + damped
    for i in range(PIVOTS):
        y[i] = g_ref[:, i * PIVOT : (i + 1) * PIVOT].astype(f32)

    for k in range(PIVOTS):
        invert(c[spot(k, k)], p.at[k], m, x, r)
        for i in range(k + 1, PIVOTS):
            low[i, k] = dot(c[spot(i, k)], p[k])
            low_high[spot(i, k)], low_low[spot(i, k)] = split(low[i, k])
        for i in range(k + 1, PIVOTS):
            for j in range(k + 1, i + 1):
                c[spot(i, j)] = c[spot(i, j)] - dot(low[i, k], c[spot(j, k)], ((1,), (1,)))
        halves = split(y[k])
        for i in range(k + 1, PIVOTS):
            y[i] = y[i] - dot3(halves, (low_high[spot(i, k)], low_low[spot(i, k)]), ((1,), (1,)))
    scale = 1.0 / math.sqrt(WIDTH * 8)
    solved = {}
    for k in range(PIVOTS - 1, -1, -1):
        h = dot3(split(y[k]), split(p[k]))
        for i in range(k + 1, PIVOTS):
            h = h - dot3(solved[i], (low_high[spot(i, k)], low_low[spot(i, k)]))
        solved[k] = split(h)
        h = h * scale
        high = h.astype(bf16)
        rest = (h - high.astype(f32)).astype(bf16)
        for block in range(DOC_DEV // BLOCK):
            out_ref[2 * block * BLOCK : (2 * block + 1) * BLOCK, k * PIVOT : (k + 1) * PIVOT] = high[block * BLOCK : (block + 1) * BLOCK]
            out_ref[(2 * block + 1) * BLOCK : (2 * block + 2) * BLOCK, k * PIVOT : (k + 1) * PIVOT] = rest[block * BLOCK : (block + 1) * BLOCK]


def solve(place, level, mine, other, g):
    smem, vmem = pl.BlockSpec(memory_space=pltpu.SMEM), pl.BlockSpec(memory_space=pltpu.VMEM)
    return pl.pallas_call(
        solve_kernel,
        out_shape=jax.ShapeDtypeStruct((2 * DOC_DEV, WIDTH), bf16),
        in_specs=[smem, smem] + [vmem] * 9,
        out_specs=vmem,
        scratch_shapes=[
            pltpu.VMEM((2 * HALF_ROWS, BLOCK), f32),
            pltpu.VMEM((10, PIVOT, PIVOT), f32),
            pltpu.VMEM((10, PIVOT, PIVOT), bf16),
            pltpu.VMEM((10, PIVOT, PIVOT), bf16),
            pltpu.VMEM((PIVOTS, PIVOT, PIVOT), f32),
            pltpu.VMEM((PIVOTS, DOC_DEV, PIVOT), f32),
            pltpu.VMEM((PIVOT, PIVOT), f32),
            pltpu.VMEM((PIVOT, PIVOT), f32),
            pltpu.VMEM((PIVOT, PIVOT), f32),
        ],
        compiler_params=pltpu.CompilerParams(vmem_limit_bytes=26 * 2**20),
        cost_estimate=pl.CostEstimate(flops=10**6, bytes_accessed=2**10, transcendentals=0),
    )(place, level, *mine, *other, g)


def products(h_ref, rows, held, place):
    both = dot16(h_ref[...], rows, ((1,), (1,)))
    for a in range(BLOCKS_DEV):
        tile = both[2 * a * BLOCK : (2 * a + 1) * BLOCK] + both[(2 * a + 1) * BLOCK : (2 * a + 2) * BLOCK]
        tile = tile.astype(bf16)
        held[a, place] = tile[:, :BLOCK]
        held[a, place + 1] = tile[:, BLOCK:]


def join(near_ref, last_ref, up_ref, joined):
    joined[:NEAR, :] = near_ref[...]
    joined[NEAR : DOC_DEV + UP, :] = last_ref[...]
    joined[DOC_DEV + UP :, :] = up_ref[...]


def first_kernel(place_ref, h_ref, sibling_ref, near_ref, last_ref, up_ref, held, joined):
    @pl.when(place_ref[2] == 0)
    def _():
        for n in range(2):
            products(h_ref, sibling_ref[n * 256 : (n + 1) * 256, :], held, 2 * n)

    join(near_ref, last_ref, up_ref, joined)
    for n in range(4):
        products(h_ref, joined[n * 256 : (n + 1) * 256, :], held, 4 + 2 * n)


def second_kernel(pairs_ref, place_ref, h_ref, early, near_ref, last_ref, up_ref, *refs):
    outs, (held, joined) = refs[:6], refs[6:]
    core = place_ref[2]
    me = place_ref[0] * 8 + place_ref[1] * 2 + core
    join(near_ref, last_ref, up_ref, joined)
    for n in range(2):
        products(h_ref, joined[n * 256 : (n + 1) * 256, :], held, 2 * n)

    @pl.when(core == 1)
    def _():
        for n in range(2, 4):
            products(h_ref, joined[n * 256 : (n + 1) * 256, :], held, 2 * n)

    def tile(n):
        first = jnp.clip(pairs_ref[0, n] - me * BLOCKS_DEV, 0, BLOCKS_DEV - 1)
        second = pairs_ref[1, n]
        ahead = jnp.maximum(second, 0) - me * BLOCKS_DEV
        ahead = jnp.where(ahead < 0, ahead + 32 * BLOCKS_DEV, ahead)
        ahead = jnp.clip(ahead, BLOCKS_DEV, (REACH + 1) * BLOCKS_DEV - 1)
        distance, column = lax.shift_right_logical(ahead, 2), jnp.bitwise_and(ahead, 3)
        even, odd = distance % 2 == 0, distance % 2 == 1
        passed_on = jnp.where(core == 0, distance == 3, odd)
        own = jnp.where(odd, 0, jnp.where(distance == 2, 1, 2))
        other = jnp.where(jnp.logical_and(core == 1, distance == 3), 1, 0)
        index = jnp.where(passed_on, other, own) * BLOCKS_DEV + column
        live = second >= 0
        value = jnp.where(passed_on, held[first, jnp.minimum(index, 7)], early[first, index])
        return jnp.where(live, value, jnp.zeros_like(value))

    y, z = place_ref[3], place_ref[4]
    for s in range(4):
        for zr in range(2):
            start = (((y + s) % 4) * 2 + (z + zr) % 2) * 8
            for j in range(4):
                outs[s][4 * zr + j] = tile(start + j)
                outs[4 + zr][4 * s + j] = tile(start + 4 + j)


def layer_tiles(pairs, place, h, pieces, passed):
    vmem, smem = pl.BlockSpec(memory_space=pltpu.VMEM), pl.BlockSpec(memory_space=pltpu.SMEM)
    params = pltpu.CompilerParams(vmem_limit_bytes=18 * 2**20)
    cost = pl.CostEstimate(flops=10**9, bytes_accessed=2**20, transcendentals=0)
    early = pl.pallas_call(
        first_kernel,
        out_shape=jax.ShapeDtypeStruct((BLOCKS_DEV, 3 * BLOCKS_DEV, BLOCK, BLOCK), bf16),
        in_specs=[smem] + [vmem] * 5,
        out_specs=vmem,
        scratch_shapes=[pltpu.VMEM((2 * DOC_DEV, WIDTH), bf16)],
        compiler_params=params,
        cost_estimate=cost,
    )(place, h, *pieces)
    return pl.pallas_call(
        second_kernel,
        out_shape=[jax.ShapeDtypeStruct((count, BLOCK, BLOCK), bf16) for count in (8, 8, 8, 8, 16, 16)],
        in_specs=[smem, smem] + [vmem] * 5,
        out_specs=[vmem] * 6,
        scratch_shapes=[
            pltpu.VMEM((BLOCKS_DEV, 2 * BLOCKS_DEV, BLOCK, BLOCK), bf16),
            pltpu.VMEM((2 * DOC_DEV, WIDTH), bf16),
        ],
        compiler_params=params,
        cost_estimate=cost,
    )(pairs, place, h, early, *passed)


def sum_layers(rows, whole):
    rows_in = [rows[0]] + [move_layer(rows[s], dy=s) for s in (1, 2, 3)]
    whole_in = move_layer(whole[1], dz=1)
    rows_sum = sum(value.astype(f32) for value in rows_in)
    whole_sum = whole[0].astype(f32) + whole_in.astype(f32)
    rows_last = move_layer(rows_sum[4:].astype(bf16), dz=1)
    cut = [whole_sum[4 * s : 4 * s + 4] for s in range(4)]
    whole_last = [move_layer(cut[s].astype(bf16), dy=s) for s in (1, 2, 3)]
    return jnp.concatenate(
        [rows_sum[:4] + rows_last.astype(f32), cut[0] + sum(value.astype(f32) for value in whole_last)]
    )


def scatter(part, position, rows, axis):
    cut = [lax.dynamic_slice_in_dim(part, ((position + s) % 4) * rows, rows) for s in range(4)]
    return [cut[0]] + [move(cut[s], **{axis: s}) for s in (1, 2, 3)]


def gather(part, axis):
    return [part] + [move(part, **{axis: -s}) for s in (1, 2, 3)]


def shards(grads, damping_level, pair_blocks):
    g = grads[0]
    me = lax.axis_index("dp")
    mine_x, mine_z, core = me // 8, (me // 2) % 4, me % 2
    early_near, early_turned = move(g[:EARLY], chips=-1), move_up(g[UP : UP + EARLY])
    sibling = move(g, dcore=1)

    part = covariance_half(g, sibling, core)
    cut = scatter(part, mine_x, X_ROWS, "dx")
    *cut, early_near, early_turned, rest = lax.optimization_barrier((*cut, early_near, early_turned, g))
    late_near, late_turned = move(g[EARLY:NEAR], chips=-1), move_up(g[UP + EARLY :])
    last = carry(jnp.concatenate([rest[NEAR:], early_near[:UP]]))
    cut = scatter(cut[0] + cut[1] + cut[2] + cut[3], mine_z, Z_ROWS, "dz")
    *cut, late_near, late_turned = lax.optimization_barrier((*cut, late_near, late_turned))
    near_0, turned = jnp.concatenate([early_near, late_near]), jnp.concatenate([early_turned, late_turned])
    part = jnp.concatenate(gather(cut[0] + cut[1] + cut[2] + cut[3], "dz"))
    part, near_0, turned, last = lax.optimization_barrier((part, near_0, turned, last))
    last = move(last, dz=-1)
    far_up = move(turned, dz=1)
    near_0_other = move(near_0, dcore=1)
    parts = gather(part, "dx")
    others = [move(part, dcore=1) for part in parts]
    layer = lax.axis_index("layer")
    place = jnp.stack([mine_x, mine_z, core, layer // 2, layer % 2]).astype(jnp.int32)
    h = solve(place, damping_level, parts, others, g)
    h, last, far_up = lax.optimization_barrier((h, last, far_up))
    last_other, far_up_other = move(last, dcore=1), move(far_up, dcore=1)
    rows_and_whole = layer_tiles(
        pair_blocks.T, place, h, (sibling, near_0, last, far_up), (near_0_other, last_other, far_up_other)
    )
    return sum_layers(rows_and_whole[:4], rows_and_whole[4:])


def solution(mesh):
    return jax.shard_map(
        shards,
        mesh=mesh,
        in_specs=(P("layer", "dp", None), P("layer"), P("dp", None)),
        out_specs=P(("dp", "layer"), None, None),
        check_vma=False,
    )
```

```python
import math

import jax
import jax.numpy as jnp
from jax import lax
from jax.experimental import pallas as pl
from jax.experimental.pallas import tpu as pltpu
from jax.sharding import PartitionSpec as P

BLOCK = 128
PIVOT = 256
PIVOTS = 4
WIDTH = PIVOT * PIVOTS
DOC_DEV = 512
DOCS = 16384
REACH = 4
HALF_ROWS = 18 * BLOCK
X_ROWS = HALF_ROWS // 4
Z_ROWS = X_ROWS // 4
BLOCKS_DEV = 4
NEAR = 320
EARLY = 256
UP = 192
TOLERANCE = 0.03
MAX_STEPS = 60
OFF_PLACE = {(1, 0): (0, 0), (2, 0): (0, 1), (3, 0): (0, 2), (2, 1): (1, 0), (3, 1): (1, 1), (3, 2): (1, 2)}

f32 = jnp.float32
bf16 = jnp.bfloat16


def dot(a, b, contract=((1,), (0,))):
    return lax.dot_general(
        a, b, (contract, ((), ())), precision=lax.Precision.HIGHEST, preferred_element_type=f32
    )


def dot16(a, b, contract=((1,), (0,))):
    return lax.dot_general(a, b, (contract, ((), ())), preferred_element_type=f32)


def split(value):
    high = value.astype(bf16)
    return high, (value - high.astype(f32)).astype(bf16)


def dot3(a, b, contract=((1,), (0,))):
    (a_high, a_low), (b_high, b_low) = a, b
    return dot16(a_high, b_high, contract) + (dot16(a_high, b_low, contract) + dot16(a_low, b_high, contract))


def split(value):
    high = value.astype(bf16)
    return high, (value - high.astype(f32)).astype(bf16)


def dot3(a, b, contract=((1,), (0,))):
    (a_high, a_low), (b_high, b_low) = a, b
    return dot16(a_high, b_high, contract) + (dot16(a_high, b_low, contract) + dot16(a_low, b_high, contract))


def move(value, dx=0, dz=0, dcore=0, chips=0):
    pairs = []
    for i in range(32):
        x, z, core = i // 8, (i // 2) % 4, i % 2
        chip = ((x + dx) % 4) * 4 + (z + dz) % 4
        pairs.append((i, ((chip + chips) % 16) * 2 + (core + dcore) % 2))
    return lax.ppermute(value, "dp", pairs)


def move_up(value):
    pairs = []
    for i in range(32):
        x, z, core = i // 8, (i // 2) % 4, i % 2
        pairs.append((i, ((x - (z < 2)) % 4) * 8 + (z + 1) % 4 * 2 + core))
    return lax.ppermute(value, "dp", pairs)


def carry(value):
    pairs = []
    for i in range(32):
        x, z, core = i // 8, (i // 2) % 4, i % 2
        pairs.append((i, ((x - (z == 0)) % 4) * 8 + z * 2 + core))
    return lax.ppermute(value, "dp", pairs)


def move_layer(value, dy=0, dz=0):
    pairs = [(i, ((i // 2 + dy) % 4) * 2 + (i + dz) % 2) for i in range(8)]
    return lax.ppermute(value, "layer", pairs)


def covariance_kernel(index_ref, g_ref, s_ref, out_ref):
    def product(place):
        i = pl.multiple_of(index_ref[2 * place] * PIVOT, PIVOT)
        j = pl.multiple_of(index_ref[2 * place + 1] * PIVOT, PIVOT)
        return dot16(g_ref[:, pl.ds(i, PIVOT)], g_ref[:, pl.ds(j, PIVOT)], ((0,), (0,))) + dot16(
            s_ref[:, pl.ds(i, PIVOT)], s_ref[:, pl.ds(j, PIVOT)], ((0,), (0,))
        )

    row = 0
    for place in range(5):
        block = product(place)
        for r, c in ((0, 0), (0, 1), (1, 0), (1, 1)):
            if place >= 3 and (r, c) == (0, 1):
                continue
            out_ref[row : row + BLOCK, :] = block[r * BLOCK : (r + 1) * BLOCK, c * BLOCK : (c + 1) * BLOCK]
            row += BLOCK


def covariance_half(g, sibling, core):
    first = jnp.array([1, 0, 2, 0, 3, 0, 0, 0, 1, 1], jnp.int32)
    second = jnp.array([2, 1, 3, 1, 3, 2, 2, 2, 3, 3], jnp.int32)
    index = jnp.where(core == 0, first, second)
    return pl.pallas_call(
        covariance_kernel,
        out_shape=jax.ShapeDtypeStruct((HALF_ROWS, BLOCK), f32),
        in_specs=[
            pl.BlockSpec(memory_space=pltpu.SMEM),
            pl.BlockSpec(memory_space=pltpu.VMEM),
            pl.BlockSpec(memory_space=pltpu.VMEM),
        ],
        out_specs=pl.BlockSpec(memory_space=pltpu.VMEM),
        compiler_params=pltpu.CompilerParams(vmem_limit_bytes=12 * 2**20),
        cost_estimate=pl.CostEstimate(flops=10**6, bytes_accessed=2**10, transcendentals=0),
    )(index, g, sibling)


def norm(r):
    return jnp.max(jnp.sum(jnp.abs(r), axis=1, keepdims=True))


def invert(a, p_ref, m_ref, x_ref, r_ref):
    rows = lax.broadcasted_iota(jnp.int32, (PIVOT, PIVOT), 0)
    cols = lax.broadcasted_iota(jnp.int32, (PIVOT, PIVOT), 1)
    eye = jnp.where(rows == cols, 1.0, 0.0).astype(f32)
    diagonal = a * eye
    scale_row = lax.rsqrt(jnp.sum(diagonal, axis=0, keepdims=True))
    scale_col = lax.rsqrt(jnp.sum(diagonal, axis=1, keepdims=True))
    m = a * scale_row * scale_col
    m_ref[...] = m
    off = eye - m
    halves = split(off)
    squared = dot3(halves, halves)
    x_ref[...] = eye + off + (squared + dot3(halves, split(squared)))

    def residual():
        r = eye - dot(m_ref[...], x_ref[...])
        r_ref[...] = r
        return norm(r)

    size = residual()

    @pl.when(jnp.logical_not(size <= TOLERANCE))
    def _():
        @pl.when(jnp.logical_not(size < 0.9))
        def _():
            step = 1.9 / norm(m_ref[...])
            x_ref[...] = step * (2.0 * eye - step * m_ref[...])

        def unfinished(carry):
            size, count = carry
            return jnp.logical_and(size > TOLERANCE, count < MAX_STEPS)

        def improve(carry):
            x_ref[...] = x_ref[...] + dot(x_ref[...], r_ref[...])
            return residual(), carry[1] + 1

        lax.while_loop(unfinished, improve, (residual(), jnp.int32(0)))

    r = split(r_ref[...])
    first = dot3(split(x_ref[...]), r)
    x = x_ref[...] + (first + dot3(split(first), r))
    p_ref[...] = x * scale_row * scale_col


def spot(i, j):
    return i * (i + 1) // 2 + j


def solve_kernel(place_ref, level_ref, *refs):
    parts, others, g_ref, out_ref = refs[:4], refs[4:8], refs[8], refs[9]
    packed, c, low_high, low_low, p, y, m, x, r = refs[10:]
    low = {}
    mine_x, mine_z, core = place_ref[0], place_ref[1], place_ref[2]
    for half, group in ((core, parts), (1 - core, others)):
        for i in range(4):
            for j in range(4):
                row = half * HALF_ROWS + ((mine_x + i) % 4) * X_ROWS + ((mine_z + j) % 4) * Z_ROWS
                row = pl.multiple_of(row, 16)
                packed[pl.ds(row, Z_ROWS), :] = group[i][j * Z_ROWS : (j + 1) * Z_ROWS, :]

    rows = lax.broadcasted_iota(jnp.int32, (PIVOT, PIVOT), 0)
    cols = lax.broadcasted_iota(jnp.int32, (PIVOT, PIVOT), 1)
    level = jnp.full((PIVOT, PIVOT), level_ref[0], jnp.int32).astype(f32)
    damped = jnp.where(rows == cols, 0.05 * jnp.exp2(level), 0.0)

    def piece(half, place):
        start = half * HALF_ROWS + place * BLOCK
        return packed[start : start + BLOCK, :] * (1.0 / DOCS)

    for (i, j), (half, place) in OFF_PLACE.items():
        for t in range(4):
            c[spot(i, j), (t // 2) * BLOCK : (t // 2 + 1) * BLOCK, (t % 2) * BLOCK : (t % 2 + 1) * BLOCK] = piece(
                half, 4 * place + t
            )
    for i in range(PIVOTS):
        half, place = i // 2, 12 + 3 * (i % 2)
        a, b, d = piece(half, place), piece(half, place + 1), piece(half, place + 2)
        top = jnp.concatenate([a, b.T], axis=1)
        bottom = jnp.concatenate([b, d], axis=1)
        c[spot(i, i)] = jnp.concatenate([top, bottom], axis=0) + damped
    for i in range(PIVOTS):
        y[i] = g_ref[:, i * PIVOT : (i + 1) * PIVOT].astype(f32)

    for k in range(PIVOTS):
        invert(c[spot(k, k)], p.at[k], m, x, r)
        for i in range(k + 1, PIVOTS):
            low[i, k] = dot(c[spot(i, k)], p[k])
            low_high[spot(i, k)], low_low[spot(i, k)] = split(low[i, k])
        for i in range(k + 1, PIVOTS):
            for j in range(k + 1, i + 1):
                c[spot(i, j)] = c[spot(i, j)] - dot(low[i, k], c[spot(j, k)], ((1,), (1,)))
        halves = split(y[k])
        for i in range(k + 1, PIVOTS):
            y[i] = y[i] - dot3(halves, (low_high[spot(i, k)], low_low[spot(i, k)]), ((1,), (1,)))
    scale = 1.0 / math.sqrt(WIDTH * 8)
    solved = {}
    for k in range(PIVOTS - 1, -1, -1):
        h = dot3(split(y[k]), split(p[k]))
        for i in range(k + 1, PIVOTS):
            h = h - dot3(solved[i], (low_high[spot(i, k)], low_low[spot(i, k)]))
        solved[k] = split(h)
        h = h * scale
        high = h.astype(bf16)
        rest = (h - high.astype(f32)).astype(bf16)
        for block in range(DOC_DEV // BLOCK):
            out_ref[2 * block * BLOCK : (2 * block + 1) * BLOCK, k * PIVOT : (k + 1) * PIVOT] = high[block * BLOCK : (block + 1) * BLOCK]
            out_ref[(2 * block + 1) * BLOCK : (2 * block + 2) * BLOCK, k * PIVOT : (k + 1) * PIVOT] = rest[block * BLOCK : (block + 1) * BLOCK]


def solve(place, level, mine, other, g):
    smem, vmem = pl.BlockSpec(memory_space=pltpu.SMEM), pl.BlockSpec(memory_space=pltpu.VMEM)
    return pl.pallas_call(
        solve_kernel,
        out_shape=jax.ShapeDtypeStruct((2 * DOC_DEV, WIDTH), bf16),
        in_specs=[smem, smem] + [vmem] * 9,
        out_specs=vmem,
        scratch_shapes=[
            pltpu.VMEM((2 * HALF_ROWS, BLOCK), f32),
            pltpu.VMEM((10, PIVOT, PIVOT), f32),
            pltpu.VMEM((10, PIVOT, PIVOT), bf16),
            pltpu.VMEM((10, PIVOT, PIVOT), bf16),
            pltpu.VMEM((PIVOTS, PIVOT, PIVOT), f32),
            pltpu.VMEM((PIVOTS, DOC_DEV, PIVOT), f32),
            pltpu.VMEM((PIVOT, PIVOT), f32),
            pltpu.VMEM((PIVOT, PIVOT), f32),
            pltpu.VMEM((PIVOT, PIVOT), f32),
        ],
        compiler_params=pltpu.CompilerParams(vmem_limit_bytes=26 * 2**20),
        cost_estimate=pl.CostEstimate(flops=10**6, bytes_accessed=2**10, transcendentals=0),
    )(place, level, *mine, *other, g)


def products(h_ref, rows, held, place):
    both = dot16(h_ref[...], rows, ((1,), (1,)))
    for a in range(BLOCKS_DEV):
        tile = both[2 * a * BLOCK : (2 * a + 1) * BLOCK] + both[(2 * a + 1) * BLOCK : (2 * a + 2) * BLOCK]
        tile = tile.astype(bf16)
        held[a, place] = tile[:, :BLOCK]
        held[a, place + 1] = tile[:, BLOCK:]


def join(near_ref, last_ref, up_ref, joined):
    joined[:NEAR, :] = near_ref[...]
    joined[NEAR : DOC_DEV + UP, :] = last_ref[...]
    joined[DOC_DEV + UP :, :] = up_ref[...]


def first_kernel(place_ref, h_ref, sibling_ref, near_ref, last_ref, up_ref, held, joined):
    @pl.when(place_ref[2] == 0)
    def _():
        for n in range(2):
            products(h_ref, sibling_ref[n * 256 : (n + 1) * 256, :], held, 2 * n)

    join(near_ref, last_ref, up_ref, joined)
    for n in range(4):
        products(h_ref, joined[n * 256 : (n + 1) * 256, :], held, 4 + 2 * n)


def second_kernel(pairs_ref, place_ref, h_ref, early, near_ref, last_ref, up_ref, *refs):
    outs, (held, joined) = refs[:6], refs[6:]
    core = place_ref[2]
    me = place_ref[0] * 8 + place_ref[1] * 2 + core
    join(near_ref, last_ref, up_ref, joined)
    for n in range(2):
        products(h_ref, joined[n * 256 : (n + 1) * 256, :], held, 2 * n)

    @pl.when(core == 1)
    def _():
        for n in range(2, 4):
            products(h_ref, joined[n * 256 : (n + 1) * 256, :], held, 2 * n)

    def tile(n):
        first = jnp.clip(pairs_ref[0, n] - me * BLOCKS_DEV, 0, BLOCKS_DEV - 1)
        second = pairs_ref[1, n]
        ahead = jnp.maximum(second, 0) - me * BLOCKS_DEV
        ahead = jnp.where(ahead < 0, ahead + 32 * BLOCKS_DEV, ahead)
        ahead = jnp.clip(ahead, BLOCKS_DEV, (REACH + 1) * BLOCKS_DEV - 1)
        distance, column = lax.shift_right_logical(ahead, 2), jnp.bitwise_and(ahead, 3)
        even, odd = distance % 2 == 0, distance % 2 == 1
        passed_on = jnp.where(core == 0, distance == 3, odd)
        own = jnp.where(odd, 0, jnp.where(distance == 2, 1, 2))
        other = jnp.where(jnp.logical_and(core == 1, distance == 3), 1, 0)
        index = jnp.where(passed_on, other, own) * BLOCKS_DEV + column
        live = second >= 0
        value = jnp.where(passed_on, held[first, jnp.minimum(index, 7)], early[first, index])
        return jnp.where(live, value, jnp.zeros_like(value))

    y, z = place_ref[3], place_ref[4]
    for s in range(4):
        for zr in range(2):
            start = (((y + s) % 4) * 2 + (z + zr) % 2) * 8
            for j in range(4):
                outs[s][4 * zr + j] = tile(start + j)
                outs[4 + zr][4 * s + j] = tile(start + 4 + j)


def layer_tiles(pairs, place, h, pieces, passed):
    vmem, smem = pl.BlockSpec(memory_space=pltpu.VMEM), pl.BlockSpec(memory_space=pltpu.SMEM)
    params = pltpu.CompilerParams(vmem_limit_bytes=18 * 2**20)
    cost = pl.CostEstimate(flops=10**9, bytes_accessed=2**20, transcendentals=0)
    early = pl.pallas_call(
        first_kernel,
        out_shape=jax.ShapeDtypeStruct((BLOCKS_DEV, 3 * BLOCKS_DEV, BLOCK, BLOCK), bf16),
        in_specs=[smem] + [vmem] * 5,
        out_specs=vmem,
        scratch_shapes=[pltpu.VMEM((2 * DOC_DEV, WIDTH), bf16)],
        compiler_params=params,
        cost_estimate=cost,
    )(place, h, *pieces)
    return pl.pallas_call(
        second_kernel,
        out_shape=[jax.ShapeDtypeStruct((count, BLOCK, BLOCK), bf16) for count in (8, 8, 8, 8, 16, 16)],
        in_specs=[smem, smem] + [vmem] * 5,
        out_specs=[vmem] * 6,
        scratch_shapes=[
            pltpu.VMEM((BLOCKS_DEV, 2 * BLOCKS_DEV, BLOCK, BLOCK), bf16),
            pltpu.VMEM((2 * DOC_DEV, WIDTH), bf16),
        ],
        compiler_params=params,
        cost_estimate=cost,
    )(pairs, place, h, early, *passed)


def sum_layers(rows, whole):
    rows_in = [rows[0]] + [move_layer(rows[s], dy=s) for s in (1, 2, 3)]
    whole_in = move_layer(whole[1], dz=1)
    rows_sum = sum(value.astype(f32) for value in rows_in)
    whole_sum = whole[0].astype(f32) + whole_in.astype(f32)
    rows_last = move_layer(rows_sum[4:].astype(bf16), dz=1)
    cut = [whole_sum[4 * s : 4 * s + 4] for s in range(4)]
    whole_last = [move_layer(cut[s].astype(bf16), dy=s) for s in (1, 2, 3)]
    return jnp.concatenate(
        [rows_sum[:4] + rows_last.astype(f32), cut[0] + sum(value.astype(f32) for value in whole_last)]
    )


def scatter(part, position, rows, axis):
    cut = [lax.dynamic_slice_in_dim(part, ((position + s) % 4) * rows, rows) for s in range(4)]
    return [cut[0]] + [move(cut[s], **{axis: s}) for s in (1, 2, 3)]


def gather(part, axis):
    return [part] + [move(part, **{axis: -s}) for s in (1, 2, 3)]


def shards(grads, damping_level, pair_blocks):
    g = grads[0]
    me = lax.axis_index("dp")
    mine_x, mine_z, core = me // 8, (me // 2) % 4, me % 2
    early_near, early_turned = move(g[:EARLY], chips=-1), move_up(g[UP : UP + EARLY])
    sibling = move(g, dcore=1)

    part = covariance_half(g, sibling, core)
    cut = scatter(part, mine_x, X_ROWS, "dx")
    *cut, early_near, early_turned, rest = lax.optimization_barrier((*cut, early_near, early_turned, g))
    late_near, late_turned = move(g[EARLY:NEAR], chips=-1), move_up(g[UP + EARLY :])
    last = carry(jnp.concatenate([rest[NEAR:], early_near[:UP]]))
    cut = scatter(cut[0] + cut[1] + cut[2] + cut[3], mine_z, Z_ROWS, "dz")
    *cut, late_near, late_turned = lax.optimization_barrier((*cut, late_near, late_turned))
    near_0, turned = jnp.concatenate([early_near, late_near]), jnp.concatenate([early_turned, late_turned])
    part = jnp.concatenate(gather(cut[0] + cut[1] + cut[2] + cut[3], "dz"))
    part, near_0, turned, last = lax.optimization_barrier((part, near_0, turned, last))
    last = move(last, dz=-1)
    far_up = move(turned, dz=1)
    near_0_other = move(near_0, dcore=1)
    parts = gather(part, "dx")
    others = [move(part, dcore=1) for part in parts]
    layer = lax.axis_index("layer")
    place = jnp.stack([mine_x, mine_z, core, layer // 2, layer % 2]).astype(jnp.int32)
    h = solve(place, damping_level, parts, others, g)
    h, last, far_up = lax.optimization_barrier((h, last, far_up))
    last_other, far_up_other = move(last, dcore=1), move(far_up, dcore=1)
    rows_and_whole = layer_tiles(
        pair_blocks.T, place, h, (sibling, near_0, last, far_up), (near_0_other, last_other, far_up_other)
    )
    return sum_layers(rows_and_whole[:4], rows_and_whole[4:])


def solution(mesh):
    return jax.shard_map(
        shards,
        mesh=mesh,
        in_specs=(P("layer", "dp", None), P("layer"), P("dp", None)),
        out_specs=P(("dp", "layer"), None, None),
        check_vma=False,
    )
```

```python
import math

import jax
import jax.numpy as jnp
from jax import lax
from jax.experimental import pallas as pl
from jax.experimental.pallas import tpu as pltpu
from jax.sharding import PartitionSpec as P

BLOCK = 128
PIVOT = 256
PIVOTS = 4
WIDTH = PIVOT * PIVOTS
DOC_DEV = 512
DOCS = 16384
REACH = 4
HALF_ROWS = 18 * BLOCK
X_ROWS = HALF_ROWS // 4
Z_ROWS = X_ROWS // 4
BLOCKS_DEV = 4
NEAR = 320
EARLY = 256
UP = 192
TOLERANCE = 0.03
MAX_STEPS = 60
OFF_PLACE = {(1, 0): (0, 0), (2, 0): (0, 1), (3, 0): (0, 2), (2, 1): (1, 0), (3, 1): (1, 1), (3, 2): (1, 2)}

f32 = jnp.float32
bf16 = jnp.bfloat16


def dot(a, b, contract=((1,), (0,))):
    return lax.dot_general(
        a, b, (contract, ((), ())), precision=lax.Precision.HIGHEST, preferred_element_type=f32
    )


def dot16(a, b, contract=((1,), (0,))):
    return lax.dot_general(a, b, (contract, ((), ())), preferred_element_type=f32)


def split(value):
    high = value.astype(bf16)
    return high, (value - high.astype(f32)).astype(bf16)


def dot3(a, b, contract=((1,), (0,))):
    (a_high, a_low), (b_high, b_low) = a, b
    return dot16(a_high, b_high, contract) + (dot16(a_high, b_low, contract) + dot16(a_low, b_high, contract))


def split(value):
    high = value.astype(bf16)
    return high, (value - high.astype(f32)).astype(bf16)


def dot3(a, b, contract=((1,), (0,))):
    (a_high, a_low), (b_high, b_low) = a, b
    return dot16(a_high, b_high, contract) + (dot16(a_high, b_low, contract) + dot16(a_low, b_high, contract))


def move(value, dx=0, dz=0, dcore=0, chips=0):
    pairs = []
    for i in range(32):
        x, z, core = i // 8, (i // 2) % 4, i % 2
        chip = ((x + dx) % 4) * 4 + (z + dz) % 4
        pairs.append((i, ((chip + chips) % 16) * 2 + (core + dcore) % 2))
    return lax.ppermute(value, "dp", pairs)


def move_up(value):
    pairs = []
    for i in range(32):
        x, z, core = i // 8, (i // 2) % 4, i % 2
        pairs.append((i, ((x - (z < 2)) % 4) * 8 + (z + 1) % 4 * 2 + core))
    return lax.ppermute(value, "dp", pairs)


def carry(value):
    pairs = []
    for i in range(32):
        x, z, core = i // 8, (i // 2) % 4, i % 2
        pairs.append((i, ((x - (z == 0)) % 4) * 8 + z * 2 + core))
    return lax.ppermute(value, "dp", pairs)


def move_layer(value, dy=0, dz=0):
    pairs = [(i, ((i // 2 + dy) % 4) * 2 + (i + dz) % 2) for i in range(8)]
    return lax.ppermute(value, "layer", pairs)


def covariance_kernel(index_ref, g_ref, s_ref, out_ref):
    def product(place):
        i = pl.multiple_of(index_ref[2 * place] * PIVOT, PIVOT)
        j = pl.multiple_of(index_ref[2 * place + 1] * PIVOT, PIVOT)
        return dot16(g_ref[:, pl.ds(i, PIVOT)], g_ref[:, pl.ds(j, PIVOT)], ((0,), (0,))) + dot16(
            s_ref[:, pl.ds(i, PIVOT)], s_ref[:, pl.ds(j, PIVOT)], ((0,), (0,))
        )

    row = 0
    for place in range(5):
        block = product(place)
        for r, c in ((0, 0), (0, 1), (1, 0), (1, 1)):
            if place >= 3 and (r, c) == (0, 1):
                continue
            out_ref[row : row + BLOCK, :] = block[r * BLOCK : (r + 1) * BLOCK, c * BLOCK : (c + 1) * BLOCK]
            row += BLOCK


def covariance_half(g, sibling, core):
    first = jnp.array([1, 0, 2, 0, 3, 0, 0, 0, 1, 1], jnp.int32)
    second = jnp.array([2, 1, 3, 1, 3, 2, 2, 2, 3, 3], jnp.int32)
    index = jnp.where(core == 0, first, second)
    return pl.pallas_call(
        covariance_kernel,
        out_shape=jax.ShapeDtypeStruct((HALF_ROWS, BLOCK), f32),
        in_specs=[
            pl.BlockSpec(memory_space=pltpu.SMEM),
            pl.BlockSpec(memory_space=pltpu.VMEM),
            pl.BlockSpec(memory_space=pltpu.VMEM),
        ],
        out_specs=pl.BlockSpec(memory_space=pltpu.VMEM),
        compiler_params=pltpu.CompilerParams(vmem_limit_bytes=12 * 2**20),
        cost_estimate=pl.CostEstimate(flops=10**6, bytes_accessed=2**10, transcendentals=0),
    )(index, g, sibling)


def norm(r):
    return jnp.max(jnp.sum(jnp.abs(r), axis=1, keepdims=True))


def invert(a, p_ref, m_ref, x_ref, r_ref):
    rows = lax.broadcasted_iota(jnp.int32, (PIVOT, PIVOT), 0)
    cols = lax.broadcasted_iota(jnp.int32, (PIVOT, PIVOT), 1)
    eye = jnp.where(rows == cols, 1.0, 0.0).astype(f32)
    diagonal = a * eye
    scale_row = lax.rsqrt(jnp.sum(diagonal, axis=0, keepdims=True))
    scale_col = lax.rsqrt(jnp.sum(diagonal, axis=1, keepdims=True))
    m = a * scale_row * scale_col
    m_ref[...] = m
    off = eye - m
    rough = off.astype(bf16)
    squared = dot16(rough, rough)
    x_ref[...] = eye + off + (squared + dot16(rough, squared.astype(bf16)))

    def residual():
        r = eye - dot(m_ref[...], x_ref[...])
        r_ref[...] = r
        return norm(r)

    size = residual()

    @pl.when(jnp.logical_not(size <= TOLERANCE))
    def _():
        @pl.when(jnp.logical_not(size < 0.9))
        def _():
            step = 1.9 / norm(m_ref[...])
            x_ref[...] = step * (2.0 * eye - step * m_ref[...])

        def unfinished(carry):
            size, count = carry
            return jnp.logical_and(size > TOLERANCE, count < MAX_STEPS)

        def improve(carry):
            x_ref[...] = x_ref[...] + dot(x_ref[...], r_ref[...])
            return residual(), carry[1] + 1

        lax.while_loop(unfinished, improve, (residual(), jnp.int32(0)))

    r = split(r_ref[...])
    first = dot3(split(x_ref[...]), r)
    x = x_ref[...] + (first + dot3(split(first), r))
    p_ref[...] = x * scale_row * scale_col


def spot(i, j):
    return i * (i + 1) // 2 + j


def solve_kernel(place_ref, level_ref, *refs):
    parts, others, g_ref, out_ref = refs[:4], refs[4:8], refs[8], refs[9]
    packed, c, low_high, low_low, p, y, m, x, r = refs[10:]
    low = {}
    mine_x, mine_z, core = place_ref[0], place_ref[1], place_ref[2]
    for half, group in ((core, parts), (1 - core, others)):
        for i in range(4):
            for j in range(4):
                row = half * HALF_ROWS + ((mine_x + i) % 4) * X_ROWS + ((mine_z + j) % 4) * Z_ROWS
                row = pl.multiple_of(row, 16)
                packed[pl.ds(row, Z_ROWS), :] = group[i][j * Z_ROWS : (j + 1) * Z_ROWS, :]

    rows = lax.broadcasted_iota(jnp.int32, (PIVOT, PIVOT), 0)
    cols = lax.broadcasted_iota(jnp.int32, (PIVOT, PIVOT), 1)
    level = jnp.full((PIVOT, PIVOT), level_ref[0], jnp.int32).astype(f32)
    damped = jnp.where(rows == cols, 0.05 * jnp.exp2(level), 0.0)

    def piece(half, place):
        start = half * HALF_ROWS + place * BLOCK
        return packed[start : start + BLOCK, :] * (1.0 / DOCS)

    for (i, j), (half, place) in OFF_PLACE.items():
        for t in range(4):
            c[spot(i, j), (t // 2) * BLOCK : (t // 2 + 1) * BLOCK, (t % 2) * BLOCK : (t % 2 + 1) * BLOCK] = piece(
                half, 4 * place + t
            )
    for i in range(PIVOTS):
        half, place = i // 2, 12 + 3 * (i % 2)
        a, b, d = piece(half, place), piece(half, place + 1), piece(half, place + 2)
        top = jnp.concatenate([a, b.T], axis=1)
        bottom = jnp.concatenate([b, d], axis=1)
        c[spot(i, i)] = jnp.concatenate([top, bottom], axis=0) + damped
    for i in range(PIVOTS):
        y[i] = g_ref[:, i * PIVOT : (i + 1) * PIVOT].astype(f32)

    for k in range(PIVOTS):
        invert(c[spot(k, k)], p.at[k], m, x, r)
        for i in range(k + 1, PIVOTS):
            low[i, k] = dot(c[spot(i, k)], p[k])
            low_high[spot(i, k)], low_low[spot(i, k)] = split(low[i, k])
        for i in range(k + 1, PIVOTS):
            for j in range(k + 1, i + 1):
                c[spot(i, j)] = c[spot(i, j)] - dot(low[i, k], c[spot(j, k)], ((1,), (1,)))
        halves = split(y[k])
        for i in range(k + 1, PIVOTS):
            if k == 0:
                term = dot16(halves[0], low_high[spot(i, k)], ((1,), (1,))) + dot16(
                    halves[0], low_low[spot(i, k)], ((1,), (1,))
                )
            else:
                term = dot3(halves, (low_high[spot(i, k)], low_low[spot(i, k)]), ((1,), (1,)))
            y[i] = y[i] - term
    scale = 1.0 / math.sqrt(WIDTH * 8)
    solved = {}
    for k in range(PIVOTS - 1, -1, -1):
        h = dot3(split(y[k]), split(p[k]))
        for i in range(k + 1, PIVOTS):
            h = h - dot3(solved[i], (low_high[spot(i, k)], low_low[spot(i, k)]))
        solved[k] = split(h)
        h = h * scale
        high = h.astype(bf16)
        rest = (h - high.astype(f32)).astype(bf16)
        for block in range(DOC_DEV // BLOCK):
            out_ref[2 * block * BLOCK : (2 * block + 1) * BLOCK, k * PIVOT : (k + 1) * PIVOT] = high[block * BLOCK : (block + 1) * BLOCK]
            out_ref[(2 * block + 1) * BLOCK : (2 * block + 2) * BLOCK, k * PIVOT : (k + 1) * PIVOT] = rest[block * BLOCK : (block + 1) * BLOCK]


def solve(place, level, mine, other, g):
    smem, vmem = pl.BlockSpec(memory_space=pltpu.SMEM), pl.BlockSpec(memory_space=pltpu.VMEM)
    return pl.pallas_call(
        solve_kernel,
        out_shape=jax.ShapeDtypeStruct((2 * DOC_DEV, WIDTH), bf16),
        in_specs=[smem, smem] + [vmem] * 9,
        out_specs=vmem,
        scratch_shapes=[
            pltpu.VMEM((2 * HALF_ROWS, BLOCK), f32),
            pltpu.VMEM((10, PIVOT, PIVOT), f32),
            pltpu.VMEM((10, PIVOT, PIVOT), bf16),
            pltpu.VMEM((10, PIVOT, PIVOT), bf16),
            pltpu.VMEM((PIVOTS, PIVOT, PIVOT), f32),
            pltpu.VMEM((PIVOTS, DOC_DEV, PIVOT), f32),
            pltpu.VMEM((PIVOT, PIVOT), f32),
            pltpu.VMEM((PIVOT, PIVOT), f32),
            pltpu.VMEM((PIVOT, PIVOT), f32),
        ],
        compiler_params=pltpu.CompilerParams(vmem_limit_bytes=26 * 2**20),
        cost_estimate=pl.CostEstimate(flops=10**6, bytes_accessed=2**10, transcendentals=0),
    )(place, level, *mine, *other, g)


def products(h_ref, rows, held, place):
    both = dot16(h_ref[...], rows, ((1,), (1,)))
    for a in range(BLOCKS_DEV):
        tile = both[2 * a * BLOCK : (2 * a + 1) * BLOCK] + both[(2 * a + 1) * BLOCK : (2 * a + 2) * BLOCK]
        tile = tile.astype(bf16)
        held[a, place] = tile[:, :BLOCK]
        held[a, place + 1] = tile[:, BLOCK:]


def join(near_ref, last_ref, up_ref, joined):
    joined[:NEAR, :] = near_ref[...]
    joined[NEAR : DOC_DEV + UP, :] = last_ref[...]
    joined[DOC_DEV + UP :, :] = up_ref[...]


def first_kernel(place_ref, h_ref, sibling_ref, near_ref, last_ref, up_ref, held, joined):
    @pl.when(place_ref[2] == 0)
    def _():
        for n in range(2):
            products(h_ref, sibling_ref[n * 256 : (n + 1) * 256, :], held, 2 * n)

    join(near_ref, last_ref, up_ref, joined)
    for n in range(4):
        products(h_ref, joined[n * 256 : (n + 1) * 256, :], held, 4 + 2 * n)


def second_kernel(pairs_ref, place_ref, h_ref, early, near_ref, last_ref, up_ref, *refs):
    outs, (held, joined) = refs[:6], refs[6:]
    core = place_ref[2]
    me = place_ref[0] * 8 + place_ref[1] * 2 + core
    join(near_ref, last_ref, up_ref, joined)
    for n in range(2):
        products(h_ref, joined[n * 256 : (n + 1) * 256, :], held, 2 * n)

    @pl.when(core == 1)
    def _():
        for n in range(2, 4):
            products(h_ref, joined[n * 256 : (n + 1) * 256, :], held, 2 * n)

    def tile(n):
        first = jnp.clip(pairs_ref[0, n] - me * BLOCKS_DEV, 0, BLOCKS_DEV - 1)
        second = pairs_ref[1, n]
        ahead = jnp.maximum(second, 0) - me * BLOCKS_DEV
        ahead = jnp.where(ahead < 0, ahead + 32 * BLOCKS_DEV, ahead)
        ahead = jnp.clip(ahead, BLOCKS_DEV, (REACH + 1) * BLOCKS_DEV - 1)
        distance, column = lax.shift_right_logical(ahead, 2), jnp.bitwise_and(ahead, 3)
        even, odd = distance % 2 == 0, distance % 2 == 1
        passed_on = jnp.where(core == 0, distance == 3, odd)
        own = jnp.where(odd, 0, jnp.where(distance == 2, 1, 2))
        other = jnp.where(jnp.logical_and(core == 1, distance == 3), 1, 0)
        index = jnp.where(passed_on, other, own) * BLOCKS_DEV + column
        live = second >= 0
        value = jnp.where(passed_on, held[first, jnp.minimum(index, 7)], early[first, index])
        return jnp.where(live, value, jnp.zeros_like(value))

    y, z = place_ref[3], place_ref[4]
    for s in range(4):
        for zr in range(2):
            start = (((y + s) % 4) * 2 + (z + zr) % 2) * 8
            for j in range(4):
                outs[s][4 * zr + j] = tile(start + j)
                outs[4 + zr][4 * s + j] = tile(start + 4 + j)


def layer_tiles(pairs, place, h, pieces, passed):
    vmem, smem = pl.BlockSpec(memory_space=pltpu.VMEM), pl.BlockSpec(memory_space=pltpu.SMEM)
    params = pltpu.CompilerParams(vmem_limit_bytes=18 * 2**20)
    cost = pl.CostEstimate(flops=10**9, bytes_accessed=2**20, transcendentals=0)
    early = pl.pallas_call(
        first_kernel,
        out_shape=jax.ShapeDtypeStruct((BLOCKS_DEV, 3 * BLOCKS_DEV, BLOCK, BLOCK), bf16),
        in_specs=[smem] + [vmem] * 5,
        out_specs=vmem,
        scratch_shapes=[pltpu.VMEM((2 * DOC_DEV, WIDTH), bf16)],
        compiler_params=params,
        cost_estimate=cost,
    )(place, h, *pieces)
    return pl.pallas_call(
        second_kernel,
        out_shape=[jax.ShapeDtypeStruct((count, BLOCK, BLOCK), bf16) for count in (8, 8, 8, 8, 16, 16)],
        in_specs=[smem, smem] + [vmem] * 5,
        out_specs=[vmem] * 6,
        scratch_shapes=[
            pltpu.VMEM((BLOCKS_DEV, 2 * BLOCKS_DEV, BLOCK, BLOCK), bf16),
            pltpu.VMEM((2 * DOC_DEV, WIDTH), bf16),
        ],
        compiler_params=params,
        cost_estimate=cost,
    )(pairs, place, h, early, *passed)


def sum_layers(rows, whole):
    rows_in = [rows[0]] + [move_layer(rows[s], dy=s) for s in (1, 2, 3)]
    whole_in = move_layer(whole[1], dz=1)
    rows_sum = sum(value.astype(f32) for value in rows_in)
    whole_sum = whole[0].astype(f32) + whole_in.astype(f32)
    rows_last = move_layer(rows_sum[4:].astype(bf16), dz=1)
    cut = [whole_sum[4 * s : 4 * s + 4] for s in range(4)]
    whole_last = [move_layer(cut[s].astype(bf16), dy=s) for s in (1, 2, 3)]
    return jnp.concatenate(
        [rows_sum[:4] + rows_last.astype(f32), cut[0] + sum(value.astype(f32) for value in whole_last)]
    )


def scatter(part, position, rows, axis):
    cut = [lax.dynamic_slice_in_dim(part, ((position + s) % 4) * rows, rows) for s in range(4)]
    return [cut[0]] + [move(cut[s], **{axis: s}) for s in (1, 2, 3)]


def gather(part, axis):
    return [part] + [move(part, **{axis: -s}) for s in (1, 2, 3)]


def shards(grads, damping_level, pair_blocks):
    g = grads[0]
    me = lax.axis_index("dp")
    mine_x, mine_z, core = me // 8, (me // 2) % 4, me % 2
    early_near, early_turned = move(g[:EARLY], chips=-1), move_up(g[UP : UP + EARLY])
    sibling = move(g, dcore=1)

    part = covariance_half(g, sibling, core)
    cut = scatter(part, mine_x, X_ROWS, "dx")
    *cut, early_near, early_turned, rest = lax.optimization_barrier((*cut, early_near, early_turned, g))
    late_near, late_turned = move(g[EARLY:NEAR], chips=-1), move_up(g[UP + EARLY :])
    last = carry(jnp.concatenate([rest[NEAR:], early_near[:UP]]))
    cut = scatter(cut[0] + cut[1] + cut[2] + cut[3], mine_z, Z_ROWS, "dz")
    *cut, late_near, late_turned = lax.optimization_barrier((*cut, late_near, late_turned))
    near_0, turned = jnp.concatenate([early_near, late_near]), jnp.concatenate([early_turned, late_turned])
    part = jnp.concatenate(gather(cut[0] + cut[1] + cut[2] + cut[3], "dz"))
    part, near_0, turned, last = lax.optimization_barrier((part, near_0, turned, last))
    last = move(last, dz=-1)
    far_up = move(turned, dz=1)
    near_0_other = move(near_0, dcore=1)
    parts = gather(part, "dx")
    others = [move(part, dcore=1) for part in parts]
    layer = lax.axis_index("layer")
    place = jnp.stack([mine_x, mine_z, core, layer // 2, layer % 2]).astype(jnp.int32)
    h = solve(place, damping_level, parts, others, g)
    h, last, far_up = lax.optimization_barrier((h, last, far_up))
    last_other, far_up_other = move(last, dcore=1), move(far_up, dcore=1)
    rows_and_whole = layer_tiles(
        pair_blocks.T, place, h, (sibling, near_0, last, far_up), (near_0_other, last_other, far_up_other)
    )
    return sum_layers(rows_and_whole[:4], rows_and_whole[4:])


def solution(mesh):
    return jax.shard_map(
        shards,
        mesh=mesh,
        in_specs=(P("layer", "dp", None), P("layer"), P("dp", None)),
        out_specs=P(("dp", "layer"), None, None),
        check_vma=False,
    )
```

```python
import math

import jax
import jax.numpy as jnp
from jax import lax
from jax.experimental import pallas as pl
from jax.experimental.pallas import tpu as pltpu
from jax.sharding import PartitionSpec as P

BLOCK = 128
PIVOT = 256
PIVOTS = 4
WIDTH = PIVOT * PIVOTS
DOC_DEV = 512
DOCS = 16384
REACH = 4
HALF_ROWS = 18 * BLOCK
X_ROWS = HALF_ROWS // 4
Z_ROWS = X_ROWS // 4
BLOCKS_DEV = 4
NEAR = 320
EARLY = 288
UP = 192
TOLERANCE = 0.03
MAX_STEPS = 60
OFF_PLACE = {(1, 0): (0, 0), (2, 0): (0, 1), (3, 0): (0, 2), (2, 1): (1, 0), (3, 1): (1, 1), (3, 2): (1, 2)}

f32 = jnp.float32
bf16 = jnp.bfloat16


def dot(a, b, contract=((1,), (0,))):
    return lax.dot_general(
        a, b, (contract, ((), ())), precision=lax.Precision.HIGHEST, preferred_element_type=f32
    )


def dot16(a, b, contract=((1,), (0,))):
    return lax.dot_general(a, b, (contract, ((), ())), preferred_element_type=f32)


def split(value):
    high = value.astype(bf16)
    return high, (value - high.astype(f32)).astype(bf16)


def dot3(a, b, contract=((1,), (0,))):
    (a_high, a_low), (b_high, b_low) = a, b
    return dot16(a_high, b_high, contract) + (dot16(a_high, b_low, contract) + dot16(a_low, b_high, contract))


def split(value):
    high = value.astype(bf16)
    return high, (value - high.astype(f32)).astype(bf16)


def dot3(a, b, contract=((1,), (0,))):
    (a_high, a_low), (b_high, b_low) = a, b
    return dot16(a_high, b_high, contract) + (dot16(a_high, b_low, contract) + dot16(a_low, b_high, contract))


def move(value, dx=0, dz=0, dcore=0, chips=0):
    pairs = []
    for i in range(32):
        x, z, core = i // 8, (i // 2) % 4, i % 2
        chip = ((x + dx) % 4) * 4 + (z + dz) % 4
        pairs.append((i, ((chip + chips) % 16) * 2 + (core + dcore) % 2))
    return lax.ppermute(value, "dp", pairs)


def move_up(value):
    pairs = []
    for i in range(32):
        x, z, core = i // 8, (i // 2) % 4, i % 2
        pairs.append((i, ((x - (z < 2)) % 4) * 8 + (z + 1) % 4 * 2 + core))
    return lax.ppermute(value, "dp", pairs)


def carry(value):
    pairs = []
    for i in range(32):
        x, z, core = i // 8, (i // 2) % 4, i % 2
        pairs.append((i, ((x - (z == 0)) % 4) * 8 + z * 2 + core))
    return lax.ppermute(value, "dp", pairs)


def move_layer(value, dy=0, dz=0):
    pairs = [(i, ((i // 2 + dy) % 4) * 2 + (i + dz) % 2) for i in range(8)]
    return lax.ppermute(value, "layer", pairs)


def covariance_kernel(index_ref, g_ref, s_ref, out_ref):
    def product(place):
        i = pl.multiple_of(index_ref[2 * place] * PIVOT, PIVOT)
        j = pl.multiple_of(index_ref[2 * place + 1] * PIVOT, PIVOT)
        return dot16(g_ref[:, pl.ds(i, PIVOT)], g_ref[:, pl.ds(j, PIVOT)], ((0,), (0,))) + dot16(
            s_ref[:, pl.ds(i, PIVOT)], s_ref[:, pl.ds(j, PIVOT)], ((0,), (0,))
        )

    row = 0
    for place in range(5):
        block = product(place)
        for r, c in ((0, 0), (0, 1), (1, 0), (1, 1)):
            if place >= 3 and (r, c) == (0, 1):
                continue
            out_ref[row : row + BLOCK, :] = block[r * BLOCK : (r + 1) * BLOCK, c * BLOCK : (c + 1) * BLOCK]
            row += BLOCK


def covariance_half(g, sibling, core):
    first = jnp.array([1, 0, 2, 0, 3, 0, 0, 0, 1, 1], jnp.int32)
    second = jnp.array([2, 1, 3, 1, 3, 2, 2, 2, 3, 3], jnp.int32)
    index = jnp.where(core == 0, first, second)
    return pl.pallas_call(
        covariance_kernel,
        out_shape=jax.ShapeDtypeStruct((HALF_ROWS, BLOCK), f32),
        in_specs=[
            pl.BlockSpec(memory_space=pltpu.SMEM),
            pl.BlockSpec(memory_space=pltpu.VMEM),
            pl.BlockSpec(memory_space=pltpu.VMEM),
        ],
        out_specs=pl.BlockSpec(memory_space=pltpu.VMEM),
        compiler_params=pltpu.CompilerParams(vmem_limit_bytes=12 * 2**20),
        cost_estimate=pl.CostEstimate(flops=10**6, bytes_accessed=2**10, transcendentals=0),
    )(index, g, sibling)


def norm(r):
    return jnp.max(jnp.sum(jnp.abs(r), axis=1, keepdims=True))


def invert(a, p_ref, m_ref, x_ref, r_ref):
    rows = lax.broadcasted_iota(jnp.int32, (PIVOT, PIVOT), 0)
    cols = lax.broadcasted_iota(jnp.int32, (PIVOT, PIVOT), 1)
    eye = jnp.where(rows == cols, 1.0, 0.0).astype(f32)
    diagonal = a * eye
    scale_row = lax.rsqrt(jnp.sum(diagonal, axis=0, keepdims=True))
    scale_col = lax.rsqrt(jnp.sum(diagonal, axis=1, keepdims=True))
    m = a * scale_row * scale_col
    m_ref[...] = m
    off = eye - m
    rough = off.astype(bf16)
    squared = dot16(rough, rough)
    x_ref[...] = eye + off + (squared + dot16(rough, squared.astype(bf16)))

    def residual():
        r = eye - dot(m_ref[...], x_ref[...])
        r_ref[...] = r
        return norm(r)

    size = residual()

    @pl.when(jnp.logical_not(size <= TOLERANCE))
    def _():
        @pl.when(jnp.logical_not(size < 0.9))
        def _():
            step = 1.9 / norm(m_ref[...])
            x_ref[...] = step * (2.0 * eye - step * m_ref[...])

        def unfinished(carry):
            size, count = carry
            return jnp.logical_and(size > TOLERANCE, count < MAX_STEPS)

        def improve(carry):
            x_ref[...] = x_ref[...] + dot(x_ref[...], r_ref[...])
            return residual(), carry[1] + 1

        lax.while_loop(unfinished, improve, (residual(), jnp.int32(0)))

    r = split(r_ref[...])
    first = dot3(split(x_ref[...]), r)
    x = x_ref[...] + (first + dot3(split(first), r))
    p_ref[...] = x * scale_row * scale_col


def spot(i, j):
    return i * (i + 1) // 2 + j


def solve_kernel(place_ref, level_ref, *refs):
    parts, others, g_ref, out_ref = refs[:4], refs[4:8], refs[8], refs[9]
    packed, c, low_high, low_low, p, y, m, x, r = refs[10:]
    low = {}
    mine_x, mine_z, core = place_ref[0], place_ref[1], place_ref[2]
    for half, group in ((core, parts), (1 - core, others)):
        for i in range(4):
            for j in range(4):
                row = half * HALF_ROWS + ((mine_x + i) % 4) * X_ROWS + ((mine_z + j) % 4) * Z_ROWS
                row = pl.multiple_of(row, 16)
                packed[pl.ds(row, Z_ROWS), :] = group[i][j * Z_ROWS : (j + 1) * Z_ROWS, :]

    rows = lax.broadcasted_iota(jnp.int32, (PIVOT, PIVOT), 0)
    cols = lax.broadcasted_iota(jnp.int32, (PIVOT, PIVOT), 1)
    level = jnp.full((PIVOT, PIVOT), level_ref[0], jnp.int32).astype(f32)
    damped = jnp.where(rows == cols, 0.05 * jnp.exp2(level), 0.0)

    def piece(half, place):
        start = half * HALF_ROWS + place * BLOCK
        return packed[start : start + BLOCK, :] * (1.0 / DOCS)

    for (i, j), (half, place) in OFF_PLACE.items():
        for t in range(4):
            c[spot(i, j), (t // 2) * BLOCK : (t // 2 + 1) * BLOCK, (t % 2) * BLOCK : (t % 2 + 1) * BLOCK] = piece(
                half, 4 * place + t
            )
    for i in range(PIVOTS):
        half, place = i // 2, 12 + 3 * (i % 2)
        a, b, d = piece(half, place), piece(half, place + 1), piece(half, place + 2)
        top = jnp.concatenate([a, b.T], axis=1)
        bottom = jnp.concatenate([b, d], axis=1)
        c[spot(i, i)] = jnp.concatenate([top, bottom], axis=0) + damped
    for i in range(PIVOTS):
        y[i] = g_ref[:, i * PIVOT : (i + 1) * PIVOT].astype(f32)

    for k in range(PIVOTS):
        invert(c[spot(k, k)], p.at[k], m, x, r)
        for i in range(k + 1, PIVOTS):
            low[i, k] = dot(c[spot(i, k)], p[k])
            low_high[spot(i, k)], low_low[spot(i, k)] = split(low[i, k])
        for i in range(k + 1, PIVOTS):
            for j in range(k + 1, i + 1):
                c[spot(i, j)] = c[spot(i, j)] - dot(low[i, k], c[spot(j, k)], ((1,), (1,)))
        halves = split(y[k])
        for i in range(k + 1, PIVOTS):
            if k == 0:
                term = dot16(halves[0], low_high[spot(i, k)], ((1,), (1,))) + dot16(
                    halves[0], low_low[spot(i, k)], ((1,), (1,))
                )
            else:
                term = dot3(halves, (low_high[spot(i, k)], low_low[spot(i, k)]), ((1,), (1,)))
            y[i] = y[i] - term
    scale = 1.0 / math.sqrt(WIDTH * 8)
    solved = {}
    for k in range(PIVOTS - 1, -1, -1):
        h = dot3(split(y[k]), split(p[k]))
        for i in range(k + 1, PIVOTS):
            h = h - dot3(solved[i], (low_high[spot(i, k)], low_low[spot(i, k)]))
        solved[k] = split(h)
        h = h * scale
        high = h.astype(bf16)
        rest = (h - high.astype(f32)).astype(bf16)
        for block in range(DOC_DEV // BLOCK):
            out_ref[2 * block * BLOCK : (2 * block + 1) * BLOCK, k * PIVOT : (k + 1) * PIVOT] = high[block * BLOCK : (block + 1) * BLOCK]
            out_ref[(2 * block + 1) * BLOCK : (2 * block + 2) * BLOCK, k * PIVOT : (k + 1) * PIVOT] = rest[block * BLOCK : (block + 1) * BLOCK]


def solve(place, level, mine, other, g):
    smem, vmem = pl.BlockSpec(memory_space=pltpu.SMEM), pl.BlockSpec(memory_space=pltpu.VMEM)
    return pl.pallas_call(
        solve_kernel,
        out_shape=jax.ShapeDtypeStruct((2 * DOC_DEV, WIDTH), bf16),
        in_specs=[smem, smem] + [vmem] * 9,
        out_specs=vmem,
        scratch_shapes=[
            pltpu.VMEM((2 * HALF_ROWS, BLOCK), f32),
            pltpu.VMEM((10, PIVOT, PIVOT), f32),
            pltpu.VMEM((10, PIVOT, PIVOT), bf16),
            pltpu.VMEM((10, PIVOT, PIVOT), bf16),
            pltpu.VMEM((PIVOTS, PIVOT, PIVOT), f32),
            pltpu.VMEM((PIVOTS, DOC_DEV, PIVOT), f32),
            pltpu.VMEM((PIVOT, PIVOT), f32),
            pltpu.VMEM((PIVOT, PIVOT), f32),
            pltpu.VMEM((PIVOT, PIVOT), f32),
        ],
        compiler_params=pltpu.CompilerParams(vmem_limit_bytes=26 * 2**20),
        cost_estimate=pl.CostEstimate(flops=10**6, bytes_accessed=2**10, transcendentals=0),
    )(place, level, *mine, *other, g)


def products(h_ref, rows, held, place):
    both = dot16(h_ref[...], rows, ((1,), (1,)))
    for a in range(BLOCKS_DEV):
        tile = both[2 * a * BLOCK : (2 * a + 1) * BLOCK] + both[(2 * a + 1) * BLOCK : (2 * a + 2) * BLOCK]
        tile = tile.astype(bf16)
        held[a, place] = tile[:, :BLOCK]
        held[a, place + 1] = tile[:, BLOCK:]


def join(near_ref, last_ref, up_ref, joined):
    joined[:NEAR, :] = near_ref[...]
    joined[NEAR : DOC_DEV + UP, :] = last_ref[...]
    joined[DOC_DEV + UP :, :] = up_ref[...]


def first_kernel(place_ref, h_ref, sibling_ref, near_ref, last_ref, up_ref, held, joined):
    @pl.when(place_ref[2] == 0)
    def _():
        for n in range(2):
            products(h_ref, sibling_ref[n * 256 : (n + 1) * 256, :], held, 2 * n)

    join(near_ref, last_ref, up_ref, joined)
    for n in range(4):
        products(h_ref, joined[n * 256 : (n + 1) * 256, :], held, 4 + 2 * n)


def second_kernel(pairs_ref, place_ref, h_ref, early, near_ref, last_ref, up_ref, *refs):
    outs, (held, joined) = refs[:6], refs[6:]
    core = place_ref[2]
    me = place_ref[0] * 8 + place_ref[1] * 2 + core
    join(near_ref, last_ref, up_ref, joined)
    for n in range(2):
        products(h_ref, joined[n * 256 : (n + 1) * 256, :], held, 2 * n)

    @pl.when(core == 1)
    def _():
        for n in range(2, 4):
            products(h_ref, joined[n * 256 : (n + 1) * 256, :], held, 2 * n)

    def tile(n):
        first = jnp.clip(pairs_ref[0, n] - me * BLOCKS_DEV, 0, BLOCKS_DEV - 1)
        second = pairs_ref[1, n]
        ahead = jnp.maximum(second, 0) - me * BLOCKS_DEV
        ahead = jnp.where(ahead < 0, ahead + 32 * BLOCKS_DEV, ahead)
        ahead = jnp.clip(ahead, BLOCKS_DEV, (REACH + 1) * BLOCKS_DEV - 1)
        distance, column = lax.shift_right_logical(ahead, 2), jnp.bitwise_and(ahead, 3)
        even, odd = distance % 2 == 0, distance % 2 == 1
        passed_on = jnp.where(core == 0, distance == 3, odd)
        own = jnp.where(odd, 0, jnp.where(distance == 2, 1, 2))
        other = jnp.where(jnp.logical_and(core == 1, distance == 3), 1, 0)
        index = jnp.where(passed_on, other, own) * BLOCKS_DEV + column
        live = second >= 0
        value = jnp.where(passed_on, held[first, jnp.minimum(index, 7)], early[first, index])
        return jnp.where(live, value, jnp.zeros_like(value))

    y, z = place_ref[3], place_ref[4]
    for s in range(4):
        for zr in range(2):
            start = (((y + s) % 4) * 2 + (z + zr) % 2) * 8
            for j in range(4):
                outs[s][4 * zr + j] = tile(start + j)
                outs[4 + zr][4 * s + j] = tile(start + 4 + j)


def layer_tiles(pairs, place, h, pieces, passed):
    vmem, smem = pl.BlockSpec(memory_space=pltpu.VMEM), pl.BlockSpec(memory_space=pltpu.SMEM)
    params = pltpu.CompilerParams(vmem_limit_bytes=18 * 2**20)
    cost = pl.CostEstimate(flops=10**9, bytes_accessed=2**20, transcendentals=0)
    early = pl.pallas_call(
        first_kernel,
        out_shape=jax.ShapeDtypeStruct((BLOCKS_DEV, 3 * BLOCKS_DEV, BLOCK, BLOCK), bf16),
        in_specs=[smem] + [vmem] * 5,
        out_specs=vmem,
        scratch_shapes=[pltpu.VMEM((2 * DOC_DEV, WIDTH), bf16)],
        compiler_params=params,
        cost_estimate=cost,
    )(place, h, *pieces)
    return pl.pallas_call(
        second_kernel,
        out_shape=[jax.ShapeDtypeStruct((count, BLOCK, BLOCK), bf16) for count in (8, 8, 8, 8, 16, 16)],
        in_specs=[smem, smem] + [vmem] * 5,
        out_specs=[vmem] * 6,
        scratch_shapes=[
            pltpu.VMEM((BLOCKS_DEV, 2 * BLOCKS_DEV, BLOCK, BLOCK), bf16),
            pltpu.VMEM((2 * DOC_DEV, WIDTH), bf16),
        ],
        compiler_params=params,
        cost_estimate=cost,
    )(pairs, place, h, early, *passed)


def sum_layers(rows, whole):
    rows_in = [rows[0]] + [move_layer(rows[s], dy=s) for s in (1, 2, 3)]
    whole_in = move_layer(whole[1], dz=1)
    rows_sum = sum(value.astype(f32) for value in rows_in)
    whole_sum = whole[0].astype(f32) + whole_in.astype(f32)
    rows_last = move_layer(rows_sum[4:].astype(bf16), dz=1)
    cut = [whole_sum[4 * s : 4 * s + 4] for s in range(4)]
    whole_last = [move_layer(cut[s].astype(bf16), dy=s) for s in (1, 2, 3)]
    return jnp.concatenate(
        [rows_sum[:4] + rows_last.astype(f32), cut[0] + sum(value.astype(f32) for value in whole_last)]
    )


def scatter(part, position, rows, axis):
    cut = [lax.dynamic_slice_in_dim(part, ((position + s) % 4) * rows, rows) for s in range(4)]
    return [cut[0]] + [move(cut[s], **{axis: s}) for s in (1, 2, 3)]


def gather(part, axis):
    return [part] + [move(part, **{axis: -s}) for s in (1, 2, 3)]


def shards(grads, damping_level, pair_blocks):
    g = grads[0]
    me = lax.axis_index("dp")
    mine_x, mine_z, core = me // 8, (me // 2) % 4, me % 2
    early_near, early_turned = move(g[:EARLY], chips=-1), move_up(g[UP : UP + EARLY])
    sibling = move(g, dcore=1)

    part = covariance_half(g, sibling, core)
    cut = scatter(part, mine_x, X_ROWS, "dx")
    *cut, early_near, early_turned, rest = lax.optimization_barrier((*cut, early_near, early_turned, g))
    late_near, late_turned = move(g[EARLY:NEAR], chips=-1), move_up(g[UP + EARLY :])
    last = carry(jnp.concatenate([rest[NEAR:], early_near[:UP]]))
    cut = scatter(cut[0] + cut[1] + cut[2] + cut[3], mine_z, Z_ROWS, "dz")
    *cut, late_near, late_turned = lax.optimization_barrier((*cut, late_near, late_turned))
    near_0, turned = jnp.concatenate([early_near, late_near]), jnp.concatenate([early_turned, late_turned])
    part = jnp.concatenate(gather(cut[0] + cut[1] + cut[2] + cut[3], "dz"))
    part, near_0, turned, last = lax.optimization_barrier((part, near_0, turned, last))
    last = move(last, dz=-1)
    far_up = move(turned, dz=1)
    near_0_other = move(near_0, dcore=1)
    parts = gather(part, "dx")
    others = [move(part, dcore=1) for part in parts]
    layer = lax.axis_index("layer")
    place = jnp.stack([mine_x, mine_z, core, layer // 2, layer % 2]).astype(jnp.int32)
    h = solve(place, damping_level, parts, others, g)
    h, last, far_up = lax.optimization_barrier((h, last, far_up))
    last_other, far_up_other = move(last, dcore=1), move(far_up, dcore=1)
    rows_and_whole = layer_tiles(
        pair_blocks.T, place, h, (sibling, near_0, last, far_up), (near_0_other, last_other, far_up_other)
    )
    return sum_layers(rows_and_whole[:4], rows_and_whole[4:])


def solution(mesh):
    return jax.shard_map(
        shards,
        mesh=mesh,
        in_specs=(P("layer", "dp", None), P("layer"), P("dp", None)),
        out_specs=P(("dp", "layer"), None, None),
        check_vma=False,
    )
```

```python
import math

import jax
import jax.numpy as jnp
from jax import lax
from jax.experimental import pallas as pl
from jax.experimental.pallas import tpu as pltpu
from jax.sharding import PartitionSpec as P

BLOCK = 128
PIVOT = 256
PIVOTS = 4
WIDTH = PIVOT * PIVOTS
DOC_DEV = 512
DOCS = 16384
REACH = 4
HALF_ROWS = 18 * BLOCK
X_ROWS = HALF_ROWS // 4
Z_ROWS = X_ROWS // 4
BLOCKS_DEV = 4
NEAR = 320
EARLY = 224
UP = 192
TOLERANCE = 0.03
MAX_STEPS = 60
OFF_PLACE = {(1, 0): (0, 0), (2, 0): (0, 1), (3, 0): (0, 2), (2, 1): (1, 0), (3, 1): (1, 1), (3, 2): (1, 2)}

f32 = jnp.float32
bf16 = jnp.bfloat16


def dot(a, b, contract=((1,), (0,))):
    return lax.dot_general(
        a, b, (contract, ((), ())), precision=lax.Precision.HIGHEST, preferred_element_type=f32
    )


def dot16(a, b, contract=((1,), (0,))):
    return lax.dot_general(a, b, (contract, ((), ())), preferred_element_type=f32)


def split(value):
    high = value.astype(bf16)
    return high, (value - high.astype(f32)).astype(bf16)


def dot3(a, b, contract=((1,), (0,))):
    (a_high, a_low), (b_high, b_low) = a, b
    return dot16(a_high, b_high, contract) + (dot16(a_high, b_low, contract) + dot16(a_low, b_high, contract))


def split(value):
    high = value.astype(bf16)
    return high, (value - high.astype(f32)).astype(bf16)


def dot3(a, b, contract=((1,), (0,))):
    (a_high, a_low), (b_high, b_low) = a, b
    return dot16(a_high, b_high, contract) + (dot16(a_high, b_low, contract) + dot16(a_low, b_high, contract))


def move(value, dx=0, dz=0, dcore=0, chips=0):
    pairs = []
    for i in range(32):
        x, z, core = i // 8, (i // 2) % 4, i % 2
        chip = ((x + dx) % 4) * 4 + (z + dz) % 4
        pairs.append((i, ((chip + chips) % 16) * 2 + (core + dcore) % 2))
    return lax.ppermute(value, "dp", pairs)


def move_up(value):
    pairs = []
    for i in range(32):
        x, z, core = i // 8, (i // 2) % 4, i % 2
        pairs.append((i, ((x - (z < 2)) % 4) * 8 + (z + 1) % 4 * 2 + core))
    return lax.ppermute(value, "dp", pairs)


def carry(value):
    pairs = []
    for i in range(32):
        x, z, core = i // 8, (i // 2) % 4, i % 2
        pairs.append((i, ((x - (z == 0)) % 4) * 8 + z * 2 + core))
    return lax.ppermute(value, "dp", pairs)


def move_layer(value, dy=0, dz=0):
    pairs = [(i, ((i // 2 + dy) % 4) * 2 + (i + dz) % 2) for i in range(8)]
    return lax.ppermute(value, "layer", pairs)


def covariance_kernel(index_ref, g_ref, s_ref, out_ref):
    def product(place):
        i = pl.multiple_of(index_ref[2 * place] * PIVOT, PIVOT)
        j = pl.multiple_of(index_ref[2 * place + 1] * PIVOT, PIVOT)
        return dot16(g_ref[:, pl.ds(i, PIVOT)], g_ref[:, pl.ds(j, PIVOT)], ((0,), (0,))) + dot16(
            s_ref[:, pl.ds(i, PIVOT)], s_ref[:, pl.ds(j, PIVOT)], ((0,), (0,))
        )

    row = 0
    for place in range(5):
        block = product(place)
        for r, c in ((0, 0), (0, 1), (1, 0), (1, 1)):
            if place >= 3 and (r, c) == (0, 1):
                continue
            out_ref[row : row + BLOCK, :] = block[r * BLOCK : (r + 1) * BLOCK, c * BLOCK : (c + 1) * BLOCK]
            row += BLOCK


def covariance_half(g, sibling, core):
    first = jnp.array([1, 0, 2, 0, 3, 0, 0, 0, 1, 1], jnp.int32)
    second = jnp.array([2, 1, 3, 1, 3, 2, 2, 2, 3, 3], jnp.int32)
    index = jnp.where(core == 0, first, second)
    return pl.pallas_call(
        covariance_kernel,
        out_shape=jax.ShapeDtypeStruct((HALF_ROWS, BLOCK), f32),
        in_specs=[
            pl.BlockSpec(memory_space=pltpu.SMEM),
            pl.BlockSpec(memory_space=pltpu.VMEM),
            pl.BlockSpec(memory_space=pltpu.VMEM),
        ],
        out_specs=pl.BlockSpec(memory_space=pltpu.VMEM),
        compiler_params=pltpu.CompilerParams(vmem_limit_bytes=12 * 2**20),
        cost_estimate=pl.CostEstimate(flops=10**6, bytes_accessed=2**10, transcendentals=0),
    )(index, g, sibling)


def norm(r):
    return jnp.max(jnp.sum(jnp.abs(r), axis=1, keepdims=True))


def invert(a, p_ref, m_ref, x_ref, r_ref):
    rows = lax.broadcasted_iota(jnp.int32, (PIVOT, PIVOT), 0)
    cols = lax.broadcasted_iota(jnp.int32, (PIVOT, PIVOT), 1)
    eye = jnp.where(rows == cols, 1.0, 0.0).astype(f32)
    diagonal = a * eye
    scale_row = lax.rsqrt(jnp.sum(diagonal, axis=0, keepdims=True))
    scale_col = lax.rsqrt(jnp.sum(diagonal, axis=1, keepdims=True))
    m = a * scale_row * scale_col
    m_ref[...] = m
    off = eye - m
    rough = off.astype(bf16)
    squared = dot16(rough, rough)
    x_ref[...] = eye + off + (squared + dot16(rough, squared.astype(bf16)))

    def residual():
        r = eye - dot(m_ref[...], x_ref[...])
        r_ref[...] = r
        return norm(r)

    size = residual()

    @pl.when(jnp.logical_not(size <= TOLERANCE))
    def _():
        @pl.when(jnp.logical_not(size < 0.9))
        def _():
            step = 1.9 / norm(m_ref[...])
            x_ref[...] = step * (2.0 * eye - step * m_ref[...])

        def unfinished(carry):
            size, count = carry
            return jnp.logical_and(size > TOLERANCE, count < MAX_STEPS)

        def improve(carry):
            x_ref[...] = x_ref[...] + dot(x_ref[...], r_ref[...])
            return residual(), carry[1] + 1

        lax.while_loop(unfinished, improve, (residual(), jnp.int32(0)))

    r = split(r_ref[...])
    first = dot3(split(x_ref[...]), r)
    x = x_ref[...] + (first + dot3(split(first), r))
    p_ref[...] = x * scale_row * scale_col


def spot(i, j):
    return i * (i + 1) // 2 + j


def solve_kernel(place_ref, level_ref, *refs):
    parts, others, g_ref, out_ref = refs[:4], refs[4:8], refs[8], refs[9]
    packed, c, low_high, low_low, p, y, m, x, r = refs[10:]
    low = {}
    mine_x, mine_z, core = place_ref[0], place_ref[1], place_ref[2]
    for half, group in ((core, parts), (1 - core, others)):
        for i in range(4):
            for j in range(4):
                row = half * HALF_ROWS + ((mine_x + i) % 4) * X_ROWS + ((mine_z + j) % 4) * Z_ROWS
                row = pl.multiple_of(row, 16)
                packed[pl.ds(row, Z_ROWS), :] = group[i][j * Z_ROWS : (j + 1) * Z_ROWS, :]

    rows = lax.broadcasted_iota(jnp.int32, (PIVOT, PIVOT), 0)
    cols = lax.broadcasted_iota(jnp.int32, (PIVOT, PIVOT), 1)
    level = jnp.full((PIVOT, PIVOT), level_ref[0], jnp.int32).astype(f32)
    damped = jnp.where(rows == cols, 0.05 * jnp.exp2(level), 0.0)

    def piece(half, place):
        start = half * HALF_ROWS + place * BLOCK
        return packed[start : start + BLOCK, :] * (1.0 / DOCS)

    for (i, j), (half, place) in OFF_PLACE.items():
        for t in range(4):
            c[spot(i, j), (t // 2) * BLOCK : (t // 2 + 1) * BLOCK, (t % 2) * BLOCK : (t % 2 + 1) * BLOCK] = piece(
                half, 4 * place + t
            )
    for i in range(PIVOTS):
        half, place = i // 2, 12 + 3 * (i % 2)
        a, b, d = piece(half, place), piece(half, place + 1), piece(half, place + 2)
        top = jnp.concatenate([a, b.T], axis=1)
        bottom = jnp.concatenate([b, d], axis=1)
        c[spot(i, i)] = jnp.concatenate([top, bottom], axis=0) + damped
    for i in range(PIVOTS):
        y[i] = g_ref[:, i * PIVOT : (i + 1) * PIVOT].astype(f32)

    for k in range(PIVOTS):
        invert(c[spot(k, k)], p.at[k], m, x, r)
        for i in range(k + 1, PIVOTS):
            low[i, k] = dot(c[spot(i, k)], p[k])
            low_high[spot(i, k)], low_low[spot(i, k)] = split(low[i, k])
        for i in range(k + 1, PIVOTS):
            for j in range(k + 1, i + 1):
                c[spot(i, j)] = c[spot(i, j)] - dot(low[i, k], c[spot(j, k)], ((1,), (1,)))
        halves = split(y[k])
        for i in range(k + 1, PIVOTS):
            if k == 0:
                term = dot16(halves[0], low_high[spot(i, k)], ((1,), (1,))) + dot16(
                    halves[0], low_low[spot(i, k)], ((1,), (1,))
                )
            else:
                term = dot3(halves, (low_high[spot(i, k)], low_low[spot(i, k)]), ((1,), (1,)))
            y[i] = y[i] - term
    scale = 1.0 / math.sqrt(WIDTH * 8)
    solved = {}
    for k in range(PIVOTS - 1, -1, -1):
        h = dot3(split(y[k]), split(p[k]))
        for i in range(k + 1, PIVOTS):
            h = h - dot3(solved[i], (low_high[spot(i, k)], low_low[spot(i, k)]))
        solved[k] = split(h)
        h = h * scale
        high = h.astype(bf16)
        rest = (h - high.astype(f32)).astype(bf16)
        for block in range(DOC_DEV // BLOCK):
            out_ref[2 * block * BLOCK : (2 * block + 1) * BLOCK, k * PIVOT : (k + 1) * PIVOT] = high[block * BLOCK : (block + 1) * BLOCK]
            out_ref[(2 * block + 1) * BLOCK : (2 * block + 2) * BLOCK, k * PIVOT : (k + 1) * PIVOT] = rest[block * BLOCK : (block + 1) * BLOCK]


def solve(place, level, mine, other, g):
    smem, vmem = pl.BlockSpec(memory_space=pltpu.SMEM), pl.BlockSpec(memory_space=pltpu.VMEM)
    return pl.pallas_call(
        solve_kernel,
        out_shape=jax.ShapeDtypeStruct((2 * DOC_DEV, WIDTH), bf16),
        in_specs=[smem, smem] + [vmem] * 9,
        out_specs=vmem,
        scratch_shapes=[
            pltpu.VMEM((2 * HALF_ROWS, BLOCK), f32),
            pltpu.VMEM((10, PIVOT, PIVOT), f32),
            pltpu.VMEM((10, PIVOT, PIVOT), bf16),
            pltpu.VMEM((10, PIVOT, PIVOT), bf16),
            pltpu.VMEM((PIVOTS, PIVOT, PIVOT), f32),
            pltpu.VMEM((PIVOTS, DOC_DEV, PIVOT), f32),
            pltpu.VMEM((PIVOT, PIVOT), f32),
            pltpu.VMEM((PIVOT, PIVOT), f32),
            pltpu.VMEM((PIVOT, PIVOT), f32),
        ],
        compiler_params=pltpu.CompilerParams(vmem_limit_bytes=26 * 2**20),
        cost_estimate=pl.CostEstimate(flops=10**6, bytes_accessed=2**10, transcendentals=0),
    )(place, level, *mine, *other, g)


def products(h_ref, rows, held, place):
    both = dot16(h_ref[...], rows, ((1,), (1,)))
    for a in range(BLOCKS_DEV):
        tile = both[2 * a * BLOCK : (2 * a + 1) * BLOCK] + both[(2 * a + 1) * BLOCK : (2 * a + 2) * BLOCK]
        tile = tile.astype(bf16)
        held[a, place] = tile[:, :BLOCK]
        held[a, place + 1] = tile[:, BLOCK:]


def join(near_ref, last_ref, up_ref, joined):
    joined[:NEAR, :] = near_ref[...]
    joined[NEAR : DOC_DEV + UP, :] = last_ref[...]
    joined[DOC_DEV + UP :, :] = up_ref[...]


def first_kernel(place_ref, h_ref, sibling_ref, near_ref, last_ref, up_ref, held, joined):
    @pl.when(place_ref[2] == 0)
    def _():
        for n in range(2):
            products(h_ref, sibling_ref[n * 256 : (n + 1) * 256, :], held, 2 * n)

    join(near_ref, last_ref, up_ref, joined)
    for n in range(4):
        products(h_ref, joined[n * 256 : (n + 1) * 256, :], held, 4 + 2 * n)


def second_kernel(pairs_ref, place_ref, h_ref, early, near_ref, last_ref, up_ref, *refs):
    outs, (held, joined) = refs[:6], refs[6:]
    core = place_ref[2]
    me = place_ref[0] * 8 + place_ref[1] * 2 + core
    join(near_ref, last_ref, up_ref, joined)
    for n in range(2):
        products(h_ref, joined[n * 256 : (n + 1) * 256, :], held, 2 * n)

    @pl.when(core == 1)
    def _():
        for n in range(2, 4):
            products(h_ref, joined[n * 256 : (n + 1) * 256, :], held, 2 * n)

    def tile(n):
        first = jnp.clip(pairs_ref[0, n] - me * BLOCKS_DEV, 0, BLOCKS_DEV - 1)
        second = pairs_ref[1, n]
        ahead = jnp.maximum(second, 0) - me * BLOCKS_DEV
        ahead = jnp.where(ahead < 0, ahead + 32 * BLOCKS_DEV, ahead)
        ahead = jnp.clip(ahead, BLOCKS_DEV, (REACH + 1) * BLOCKS_DEV - 1)
        distance, column = lax.shift_right_logical(ahead, 2), jnp.bitwise_and(ahead, 3)
        even, odd = distance % 2 == 0, distance % 2 == 1
        passed_on = jnp.where(core == 0, distance == 3, odd)
        own = jnp.where(odd, 0, jnp.where(distance == 2, 1, 2))
        other = jnp.where(jnp.logical_and(core == 1, distance == 3), 1, 0)
        index = jnp.where(passed_on, other, own) * BLOCKS_DEV + column
        live = second >= 0
        value = jnp.where(passed_on, held[first, jnp.minimum(index, 7)], early[first, index])
        return jnp.where(live, value, jnp.zeros_like(value))

    y, z = place_ref[3], place_ref[4]
    for s in range(4):
        for zr in range(2):
            start = (((y + s) % 4) * 2 + (z + zr) % 2) * 8
            for j in range(4):
                outs[s][4 * zr + j] = tile(start + j)
                outs[4 + zr][4 * s + j] = tile(start + 4 + j)


def layer_tiles(pairs, place, h, pieces, passed):
    vmem, smem = pl.BlockSpec(memory_space=pltpu.VMEM), pl.BlockSpec(memory_space=pltpu.SMEM)
    params = pltpu.CompilerParams(vmem_limit_bytes=18 * 2**20)
    cost = pl.CostEstimate(flops=10**9, bytes_accessed=2**20, transcendentals=0)
    early = pl.pallas_call(
        first_kernel,
        out_shape=jax.ShapeDtypeStruct((BLOCKS_DEV, 3 * BLOCKS_DEV, BLOCK, BLOCK), bf16),
        in_specs=[smem] + [vmem] * 5,
        out_specs=vmem,
        scratch_shapes=[pltpu.VMEM((2 * DOC_DEV, WIDTH), bf16)],
        compiler_params=params,
        cost_estimate=cost,
    )(place, h, *pieces)
    return pl.pallas_call(
        second_kernel,
        out_shape=[jax.ShapeDtypeStruct((count, BLOCK, BLOCK), bf16) for count in (8, 8, 8, 8, 16, 16)],
        in_specs=[smem, smem] + [vmem] * 5,
        out_specs=[vmem] * 6,
        scratch_shapes=[
            pltpu.VMEM((BLOCKS_DEV, 2 * BLOCKS_DEV, BLOCK, BLOCK), bf16),
            pltpu.VMEM((2 * DOC_DEV, WIDTH), bf16),
        ],
        compiler_params=params,
        cost_estimate=cost,
    )(pairs, place, h, early, *passed)


def sum_layers(rows, whole):
    rows_in = [rows[0]] + [move_layer(rows[s], dy=s) for s in (1, 2, 3)]
    whole_in = move_layer(whole[1], dz=1)
    rows_sum = sum(value.astype(f32) for value in rows_in)
    whole_sum = whole[0].astype(f32) + whole_in.astype(f32)
    rows_last = move_layer(rows_sum[4:].astype(bf16), dz=1)
    cut = [whole_sum[4 * s : 4 * s + 4] for s in range(4)]
    whole_last = [move_layer(cut[s].astype(bf16), dy=s) for s in (1, 2, 3)]
    return jnp.concatenate(
        [rows_sum[:4] + rows_last.astype(f32), cut[0] + sum(value.astype(f32) for value in whole_last)]
    )


def scatter(part, position, rows, axis):
    cut = [lax.dynamic_slice_in_dim(part, ((position + s) % 4) * rows, rows) for s in range(4)]
    return [cut[0]] + [move(cut[s], **{axis: s}) for s in (1, 2, 3)]


def gather(part, axis):
    return [part] + [move(part, **{axis: -s}) for s in (1, 2, 3)]


def shards(grads, damping_level, pair_blocks):
    g = grads[0]
    me = lax.axis_index("dp")
    mine_x, mine_z, core = me // 8, (me // 2) % 4, me % 2
    early_near, early_turned = move(g[:EARLY], chips=-1), move_up(g[UP : UP + EARLY])
    sibling = move(g, dcore=1)

    part = covariance_half(g, sibling, core)
    cut = scatter(part, mine_x, X_ROWS, "dx")
    *cut, early_near, early_turned, rest = lax.optimization_barrier((*cut, early_near, early_turned, g))
    late_near, late_turned = move(g[EARLY:NEAR], chips=-1), move_up(g[UP + EARLY :])
    last = carry(jnp.concatenate([rest[NEAR:], early_near[:UP]]))
    cut = scatter(cut[0] + cut[1] + cut[2] + cut[3], mine_z, Z_ROWS, "dz")
    *cut, late_near, late_turned = lax.optimization_barrier((*cut, late_near, late_turned))
    near_0, turned = jnp.concatenate([early_near, late_near]), jnp.concatenate([early_turned, late_turned])
    part = jnp.concatenate(gather(cut[0] + cut[1] + cut[2] + cut[3], "dz"))
    part, near_0, turned, last = lax.optimization_barrier((part, near_0, turned, last))
    last = move(last, dz=-1)
    far_up = move(turned, dz=1)
    near_0_other = move(near_0, dcore=1)
    parts = gather(part, "dx")
    others = [move(part, dcore=1) for part in parts]
    layer = lax.axis_index("layer")
    place = jnp.stack([mine_x, mine_z, core, layer // 2, layer % 2]).astype(jnp.int32)
    h = solve(place, damping_level, parts, others, g)
    h, last, far_up = lax.optimization_barrier((h, last, far_up))
    last_other, far_up_other = move(last, dcore=1), move(far_up, dcore=1)
    rows_and_whole = layer_tiles(
        pair_blocks.T, place, h, (sibling, near_0, last, far_up), (near_0_other, last_other, far_up_other)
    )
    return sum_layers(rows_and_whole[:4], rows_and_whole[4:])


def solution(mesh):
    return jax.shard_map(
        shards,
        mesh=mesh,
        in_specs=(P("layer", "dp", None), P("layer"), P("dp", None)),
        out_specs=P(("dp", "layer"), None, None),
        check_vma=False,
    )
```
